256 devices in a mesh: seq: 16 (over z, core), fsdp: 16 (over x, y).
Axes of the slice: x: 4, y: 4, z: 8, core: 2. Of those that a mesh axis runs over, the one named last changes fastest.
Arguments:
- tokens: bfloat16 [16, 2048, 4096], P('fsdp', 'seq'), may hold values from -6 to 6
- queries: bfloat16 [16, 2048, 4096], P('fsdp', 'seq'), may hold values from -300 to 300, as said below
- norm_gain: float32 [4096], replicated, may hold values from 0.5 to 2
- w_key: bfloat16 [4096, 1024], P('fsdp'), may hold values from -0.09375 to 0.09375
- w_value: bfloat16 [4096, 1024], P('fsdp'), may hold values from -0.09375 to 0.09375
- block_list: int32 [16, 32, 32, 16], P('fsdp'), may hold values from -1 to 31, as said below
Outputs:
- attended: bfloat16 [16, 2048, 4096], P('fsdp', 'seq')
The draws below stay inside these ranges and needn't reach their ends.
Inputs may be any that keep to these rules, and one draw needn't show every extreme that they name: `queries`: values at most a few hundred in magnitude. `block_list`: in every row the entries that are not -1 come first; they are distinct key blocks no later than the row's query block, and the query block itself is among them. Each row lists at least min(2, its query block + 1) blocks, and in every sequence some row lists 16.
All inputs are finite; a program needn't handle non-finite values.
Results may differ from the reference program's by a relative error of at most 0.015.
The reference program's roundings to bfloat16 on the way (of `normed`, `key_rows`, `value_rows`, `query_rows` and `probs`) count: a program that leaves them out, or rounds other values in their place, can miss the bound.
Values may be sent and summed in bfloat16 or wider, within the bound.
A program may use at most 128 MiB of HBM per device.

```python
import math
import jax
import jax.numpy as jnp
from jax import lax

D = 4096
HEADS = 32
KV_HEADS = 8
HEAD_DIM = 128
KMAX = 16
SEQ_LEN = 2048
SEQS = 16
NQB = 32


def draw_queries(key, part):
    key = jax.random.fold_in(key, 3)
    draw_shape = (SEQS, SEQ_LEN, HEADS, HEAD_DIM)
    values = jax.random.truncated_normal(key, -4.0, 4.0, draw_shape, jnp.float32) * 2.5
    return values.reshape(SEQS, SEQ_LEN, HEADS * HEAD_DIM).astype(jnp.bfloat16)


def draw_block_list(key, part):
    key = jax.random.fold_in(key, 7)
    key_parts = jax.random.split(key, 5)
    counts = jax.random.randint(key_parts[0], (SEQS, HEADS), 2, KMAX + 1)
    heavy_head = jax.random.randint(key_parts[1], (SEQS,), 0, HEADS)
    counts = jnp.where(jnp.arange(HEADS)[None, :] == heavy_head[:, None], KMAX, counts)
    query_ids = jnp.arange(NQB)[:, None]
    key_ids = jnp.arange(NQB)[None, :]
    base_draw = jax.random.randint(key_parts[2], (SEQS, HEADS, NQB, NQB), 0, 1000)
    vertical = (jax.random.randint(key_parts[3], (SEQS, HEADS, 1, NQB), 0, 4) == 0).astype(jnp.int32)
    slash_pick = (jax.random.randint(key_parts[4], (SEQS, HEADS, NQB), 0, 4) == 0).astype(jnp.int32)
    offset = jnp.clip(query_ids - key_ids, 0, NQB - 1)
    slash_hit = jnp.take(slash_pick, offset, axis=2)
    priority = base_draw + 2000 * vertical + 2000 * slash_hit
    priority = priority + 4000 * (key_ids == 0).astype(jnp.int32) + 8000 * (key_ids == query_ids).astype(jnp.int32)
    priority = jnp.where(key_ids <= query_ids, priority * NQB + key_ids, -1)
    top_vals, top_ids = lax.top_k(priority, KMAX)
    limit = jnp.minimum(counts[:, :, None, None], jnp.arange(NQB)[None, None, :, None] + 1)
    live_slot = jnp.arange(KMAX)[None, None, None, :] < limit
    return jnp.where(live_slot, top_ids, -1).astype(jnp.int32)


def steps_of(stream_key, shape, shards, low, largest):
    level, own = 1.0, jax.random.fold_in(stream_key, 6)
    for axis_at, parts in shards:
        heights = jnp.exp(jax.random.uniform(jax.random.fold_in(own, axis_at), (parts,), jnp.float32, low / len(shards), largest / len(shards)))
        level = level * jnp.repeat(heights, shape[axis_at] // parts).reshape([-1 if axis == axis_at else 1 for axis in range(len(shape))])
    return level


def scatter_about(stream_key, shape, spread, most, shards=(), held_as=jnp.bfloat16):
    factor_of = steps_of(stream_key, shape, shards, -0.22, 0.18) if shards else 1.0
    entries = jax.random.normal(stream_key, shape, jnp.float32) * spread * factor_of
    return jnp.minimum(jnp.maximum(entries, -most), most).astype(held_as)


def setup_inputs(seed: int = 0) -> dict:
    key_of = jax.random.split(jax.random.key(seed), 7)
    tokens = scatter_about(key_of[0], (SEQS, SEQ_LEN, D), 1.0, 6.0, ((0, 16), (1, 16)))
    queries = draw_queries(jax.random.fold_in(key_of[6], 71), 0)
    norm_gain = jnp.clip(jnp.exp(jax.random.uniform(key_of[2], (D,), jnp.float32, math.log(0.5), math.log(2.0))), 0.5, 2.0)
    w_key = scatter_about(key_of[3], (D, KV_HEADS * HEAD_DIM), D ** -0.5, 0.09375, ((0, 16),))
    w_value = scatter_about(key_of[4], (D, KV_HEADS * HEAD_DIM), D ** -0.5, 0.09375, ((0, 16),))
    block_list = draw_block_list(jax.random.fold_in(key_of[6], 71), 0)
    return {"tokens": tokens, "queries": queries, "norm_gain": norm_gain, "w_key": w_key, "w_value": w_value, "block_list": block_list}


EPS = 1e-05
ROPE_BASE = 500000.0

def rotary(values, positions):
    width = values.shape[-1]
    half_width = width // 2
    freqs = ROPE_BASE ** (-jnp.arange(half_width, dtype=jnp.float32) * (2.0 / width))
    angles = positions.astype(jnp.float32)[:, None] * freqs[None, :]
    cosine = jnp.cos(angles)[:, None, :]
    sine = jnp.sin(angles)[:, None, :]
    first = values[..., :half_width]
    second = values[..., half_width:]
    return jnp.concatenate([first * cosine - second * sine, second * cosine + first * sine], axis=-1)

def attend_head(query_rows, key_rows, value_rows, lists):
    length, head_dim = key_rows.shape
    blocks, slot_count = lists.shape
    block_rows = length // blocks
    block_ids = jnp.maximum(lists, 0)
    key_tiles = key_rows.reshape(blocks, block_rows, head_dim)[block_ids].reshape(blocks, slot_count * block_rows, head_dim)
    value_tiles = value_rows.reshape(blocks, block_rows, head_dim)[block_ids].reshape(blocks, slot_count * block_rows, head_dim)
    query_tiles = query_rows.reshape(blocks, block_rows, head_dim)
    scores = jnp.einsum('qbd,qkd->qbk', query_tiles.astype(jnp.float32), key_tiles.astype(jnp.float32)) * (1.0 / math.sqrt(head_dim))
    key_pos = (block_ids[..., None] * block_rows + jnp.arange(block_rows, dtype=jnp.int32)).reshape(blocks, slot_count * block_rows)
    live_key = jnp.repeat(lists >= 0, block_rows, axis=-1)
    query_pos = jnp.arange(length, dtype=jnp.int32).reshape(blocks, block_rows)
    allowed = live_key[:, None, :] & (key_pos[:, None, :] <= query_pos[:, :, None])
    scores = jnp.where(allowed, scores, -jnp.inf)
    row_max = lax.optimization_barrier(jnp.max(scores, axis=-1, keepdims=True))
    weights_raw = jnp.exp(scores - row_max)
    probs = (weights_raw / lax.optimization_barrier(jnp.sum(weights_raw, axis=-1, keepdims=True))).astype(jnp.bfloat16)
    output = jnp.einsum('qbk,qkd->qbd', probs.astype(jnp.float32), value_tiles.astype(jnp.float32))
    return output.astype(jnp.bfloat16).reshape(length, head_dim)

def reference(tokens, queries, norm_gain, w_key, w_value, block_list):
    length = tokens.shape[1]
    head_count = block_list.shape[1]
    group_size = HEADS // KV_HEADS
    positions = jnp.arange(length, dtype=jnp.int32)

    def attend_sequence(packed):
        hidden_rows, query_in, patterns = packed
        wide = hidden_rows.astype(jnp.float32)
        normed = (wide * lax.rsqrt(lax.optimization_barrier(jnp.mean(wide * wide, axis=-1, keepdims=True)) + EPS) * norm_gain).astype(jnp.bfloat16)
        key_proj = jnp.dot(normed, w_key, preferred_element_type=jnp.float32)
        key_rows = rotary(key_proj.reshape(length, KV_HEADS, HEAD_DIM), positions).astype(jnp.bfloat16)
        value_rows = jnp.dot(normed, w_value, preferred_element_type=jnp.float32).astype(jnp.bfloat16).reshape(length, KV_HEADS, HEAD_DIM)
        rotated = rotary(query_in.astype(jnp.float32).reshape(length, head_count, HEAD_DIM), positions).astype(jnp.bfloat16)

        def head_output(head):
            shared = head // group_size
            query_head = lax.dynamic_index_in_dim(rotated, head, axis=1, keepdims=False)
            key_head = lax.dynamic_index_in_dim(key_rows, shared, axis=1, keepdims=False)
            value_head = lax.dynamic_index_in_dim(value_rows, shared, axis=1, keepdims=False)
            lists = lax.dynamic_index_in_dim(patterns, head, axis=0, keepdims=False)
            return attend_head(query_head, key_head, value_head, lists)
        per_head = lax.map(head_output, jnp.arange(head_count, dtype=jnp.int32))
        return per_head.transpose(1, 0, 2).reshape(length, head_count * HEAD_DIM)
    return lax.map(attend_sequence, (tokens, queries, block_list))
```

```python
import functools
import math

import jax
import jax.numpy as jnp
import numpy as np
from jax import lax
from jax.experimental import pallas as pl
from jax.experimental.pallas import tpu as pltpu
from jax.sharding import PartitionSpec as P

MESH = pl.DeviceIdType.MESH
EPS = 1e-05
ROPE_BASE = 500000.0
D = 4096
HD = 128
LENGTH = 2048
NX, NY, NZ = 4, 4, 8
KVL = 4
GROUP = 4
CHUNKS = 2 * KVL
ROWS = 128
PAIR = 2 * ROWS
BLOCK = 64
QB = PAIR // BLOCK
HIDDEN = -1e30
SCALE = math.log2(math.e) / math.sqrt(HD)


def rotary_tables():
    freqs = np.float32(ROPE_BASE) ** (
        -np.arange(HD // 2, dtype=np.float32) * np.float32(2.0 / HD)
    )
    angles = np.arange(LENGTH, dtype=np.float32)[:, None] * freqs.astype(np.float32)[None, :]
    cosine = np.cos(angles.astype(np.float64)).astype(np.float32)
    sine = np.sin(angles.astype(np.float64)).astype(np.float32)
    return np.concatenate([cosine, cosine], 1), np.concatenate([-sine, sine], 1)


def kernel(
    tokens, queries, gain, wk, wv, lists, cos_hbm, sin_hbm, out,
    wbuf, nrm, tok, gn, qin, qrot, qsend, kv, cs, sn, lst, bias, tri, sbuf, obuf,
    in_sem, own_sem, wsend, wrecv, zsend, zrecv, core_send, core_recv, osend, orecv, olocal,
):
    s = lax.axis_index("seq")
    f = lax.axis_index("fsdp")
    c = lax.rem(s, 2)
    z = lax.div(s, 2)
    x = lax.div(f, NY)
    y = lax.rem(f, NY)
    xn, xp = lax.rem(x + NX - 1, NX), lax.rem(x + 1, NX)
    yn, yp = lax.rem(y + NY - 1, NY), lax.rem(y + 1, NY)
    x2, y2 = lax.rem(x + 2, NX), lax.rem(y + 2, NY)
    x_dev = ((s, xp * NY + y), (s, xn * NY + y))
    y_dev = ((s, x * NY + yp), (s, x * NY + yn))
    z_dev = ((lax.rem(s + 2, 2 * NZ), f), (lax.rem(s + 2 * NZ - 2, 2 * NZ), f))
    partner = (s + 1 - 2 * c, f)
    row0 = pl.multiple_of(c * ROWS, ROWS)
    row1 = pl.multiple_of((1 - c) * ROWS, ROWS)

    def own_copy(t):
        kvl = lax.div(t, 2)
        cols = pl.ds(pl.multiple_of((KVL * c + kvl) * HD, HD), HD)
        return [
            pltpu.make_async_copy(w.at[:, :, cols], wbuf.at[t, x, y], own_sem.at[t])
            for w in (wk, wv)
        ]

    def start_own(t):
        key_copy, value_copy = own_copy(t)

        @pl.when(lax.rem(t, 2) == 0)
        def _():
            key_copy.start()

        @pl.when(lax.rem(t, 2) == 1)
        def _():
            value_copy.start()

    pos = pl.ds(pl.multiple_of(z * PAIR, PAIR), PAIR)
    tok_copy = pltpu.make_async_copy(tokens, tok, in_sem.at[0])
    gain_copy = pltpu.make_async_copy(gain, gn, in_sem.at[1])
    q_copy = pltpu.make_async_copy(queries, qin, in_sem.at[2])
    cos_copy = pltpu.make_async_copy(cos_hbm.at[pos, :], cs.at[0], in_sem.at[3])
    sin_copy = pltpu.make_async_copy(sin_hbm.at[pos, :], sn.at[0], in_sem.at[4])
    list_copy = pltpu.make_async_copy(lists, lst, in_sem.at[5])

    start_own(0)
    start_own(1)
    tok_copy.start()
    gain_copy.start()
    cos_copy.start()
    sin_copy.start()
    q_copy.start()
    list_copy.start()
    for t in range(2, CHUNKS):
        start_own(t)

    barrier = pltpu.get_barrier_semaphore()
    for device in (*x_dev, *y_dev, *z_dev, partner):
        pl.semaphore_signal(barrier, inc=1, device_id=device, device_id_type=MESH)
    pl.semaphore_wait(barrier, 7)

    def remote(src, dst, send, recv, device):
        return pltpu.make_async_remote_copy(
            src_ref=src, dst_ref=dst, send_sem=send, recv_sem=recv, device_id=device, device_id_type=MESH
        )

    first_dev = (x_dev, y_dev)
    second_dev = (y_dev, x_dev)

    def piece(t, half, step):
        if half == 0:
            return wbuf.at[t, (x, xn, x2, xp)[step], y, 0]
        return wbuf.at[t, x, (y, yn, y2, yp)[step], 1]

    def line(t, half, step, part=None):
        some = pl.ds(0, 4) if part is None else pl.ds(2 * part, 2)
        if half == 0:
            return wbuf.at[t, some, (y, yn, y2, yp)[step], 0]
        return wbuf.at[t, (x, xn, x2, xp)[step], some, 1]

    def rows_of(ref, part):
        return ref.at[pl.ds(64 * part, 64), :]

    def w_send(t, stage, half, d, ref, device):
        remote(ref, ref, wsend.at[t], wrecv.at[t, stage, half, d], device).start()

    def w_wait(t, stage, half, d, ref):
        remote(ref, ref, wsend.at[t], wrecv.at[t, stage, half, d], partner).wait_recv()

    def stage0(t):
        own_copy(t)[0].wait()
        for half in range(2):
            for d in range(2):
                w_send(t, 0, half, d, piece(t, half, 0), first_dev[half][d])

    def stage1(t):
        for half in range(2):
            for d, step in ((0, 1), (1, 3)):
                w_wait(t, 0, half, d, piece(t, half, step))
                w_send(t, 1, half, d, rows_of(piece(t, half, step), d), first_dev[half][d])

    def stage2(t):
        for half in range(2):
            for d in range(2):
                w_wait(t, 1, half, d, rows_of(piece(t, half, 2), d))
            for d in range(2):
                w_send(t, 2, half, d, line(t, half, 0), second_dev[half][d])

    def stage3(t):
        for half in range(2):
            for d, step in ((0, 1), (1, 3)):
                w_wait(t, 2, half, d, line(t, half, step))
                w_send(t, 3, half, d, line(t, half, step, d), second_dev[half][d])

    def stage4(t):
        for half in range(2):
            for d in range(2):
                w_wait(t, 3, half, d, line(t, half, 2, d))

    def z_slot(t, stage, d):
        if stage == 3:
            return kv.at[t, 4, pl.ds(128 * d, 128), :]
        return kv.at[t, stage + 1 if d == 0 else 7 - stage]

    def z_source(t, stage, d):
        if stage == 3:
            return kv.at[t, 3 if d == 0 else 5, pl.ds(128 * d, 128), :]
        return kv.at[t, stage if d == 0 else (8 - stage) % 8]

    def z_send(t, stage):
        for d in range(2):
            remote(
                z_source(t, stage, d), z_slot(t, stage, d), zsend.at[t], zrecv.at[t, stage, d], z_dev[d]
            ).start()

    def z_wait(t, stage):
        for d in range(2):
            ref = z_slot(t, stage, d)
            remote(ref, ref, zsend.at[t], zrecv.at[t, stage, d], partner).wait_recv()

    nrm_copy = remote(
        nrm.at[pl.ds(row0, ROWS), :], nrm.at[pl.ds(row0, ROWS), :], core_send.at[0], core_recv.at[0], partner
    )
    q_rot_copy = remote(
        qsend, qrot.at[:, :, pl.ds(row0, ROWS), :], core_send.at[1], core_recv.at[1], partner
    )
    nrm_landing = nrm.at[pl.ds(row1, ROWS), :]
    q_landing = qrot.at[:, :, pl.ds(row1, ROWS), :]

    def normalise():
        tok_copy.wait()
        gain_copy.wait()

        @pl.loop(0, ROWS // 16)
        def _(i):
            rows = pl.ds(pl.multiple_of(i * 16, 16), 16)
            wide = tok[rows, :].astype(jnp.float32)
            mean = jnp.sum(wide * wide, axis=-1, keepdims=True) * (1.0 / D)
            normed = wide * lax.rsqrt(mean + EPS) * gn[...]
            nrm[pl.ds(pl.multiple_of(row0 + i * 16, 16), 16), :] = normed.astype(jnp.bfloat16)

        nrm_copy.start()

    def rotate_queries():
        q_copy.wait()
        cos_copy.wait()
        sin_copy.wait()
        cs[1] = jnp.ones((PAIR, HD), jnp.float32)
        sn[1] = jnp.zeros((PAIR, HD), jnp.float32)

        def rotated(head):
            cols = pl.ds(pl.multiple_of(head * HD, HD), HD)
            v = qin[:, cols].astype(jnp.float32)
            turned = v * cs[0, pl.ds(row0, ROWS), :] + pltpu.roll(v, HD // 2, 1) * sn[0, pl.ds(row0, ROWS), :]
            return turned.astype(jnp.bfloat16)

        @pl.loop(0, KVL * GROUP)
        def _(h):
            kvl, g = lax.div(h, GROUP), lax.rem(h, GROUP)
            qsend[kvl, g] = rotated((1 - c) * KVL * GROUP + h)
            qrot[kvl, g, pl.ds(row0, ROWS), :] = rotated(c * KVL * GROUP + h)

        q_rot_copy.start()

    def make_bias():
        list_copy.wait()

        @pl.loop(0, NZ)
        def _(r):
            chip = lax.rem(z - r + NZ, NZ)
            blocks = lax.div(lax.broadcasted_iota(jnp.int32, (1, PAIR), 1), BLOCK) + chip * QB
            for n in range(KVL * GROUP * QB // 8):
                ids = lst[8 * n : 8 * n + 8, :]
                hit = ids[:, 0:1] == blocks
                for slot in range(1, ids.shape[1]):
                    hit = hit | (ids[:, slot : slot + 1] == blocks)
                bias[8 * n : 8 * n + 8, pl.ds(pl.multiple_of(r * PAIR, PAIR), PAIR)] = jnp.where(
                    hit, 0.0, HIDDEN
                )

        i = lax.broadcasted_iota(jnp.int32, (PAIR, PAIR), 0)
        j = lax.broadcasted_iota(jnp.int32, (PAIR, PAIR), 1)
        tri[...] = jnp.where(j <= i, 0.0, HIDDEN)

    def project(t):
        def step(k, acc):
            kx, ky = lax.div(k, 2), lax.rem(k, 2)
            w = wbuf[t, kx, pl.ds(2 * ky, 2)].reshape(512, HD)
            a = nrm[:, pl.ds(pl.multiple_of(k * 512, 512), 512)]
            return acc + jnp.dot(a, w, preferred_element_type=jnp.float32)

        acc = lax.fori_loop(0, 8, step, jnp.zeros((PAIR, HD), jnp.float32))
        kind = lax.rem(t, 2)
        kv[t, 0] = (acc * cs[kind] + pltpu.roll(acc, HD // 2, 1) * sn[kind]).astype(jnp.bfloat16)

    def attend(kvl, g):
        q = qrot[kvl, g]
        head = kvl * GROUP + g
        top = None
        for r in range(NZ):
            scores = lax.dot_general(
                q, kv[2 * kvl, r], (((1,), (1,)), ((), ())), preferred_element_type=jnp.float32
            )
            cols = slice(r * PAIR, (r + 1) * PAIR)
            hide = jnp.concatenate(
                [
                    jnp.broadcast_to(bias[pl.ds(head * QB + b, 1), cols], (BLOCK, PAIR))
                    for b in range(QB)
                ],
                0,
            )
            scores = scores * SCALE + hide
            if r == 0:
                scores = scores + tri[...]
            sbuf[:, cols] = scores
            here = jnp.maximum(scores[:, :HD], scores[:, HD:])
            top = here if top is None else jnp.maximum(top, here)
        top = jnp.max(top, axis=-1, keepdims=True)
        total, acc = None, None
        for r in range(NZ):
            p = jnp.exp2(sbuf[:, r * PAIR : (r + 1) * PAIR] - top)
            both = p[:, :HD] + p[:, HD:]
            total = both if total is None else total + both
            part = jnp.dot(p.astype(jnp.bfloat16), kv[2 * kvl + 1, r], preferred_element_type=jnp.float32)
            acc = part if acc is None else acc + part
        total = jnp.sum(total, axis=-1, keepdims=True)
        obuf[kvl, g] = (acc / total).astype(jnp.bfloat16)

    def out_cols(core, kvl, g):
        return out.at[:, pl.ds(pl.multiple_of(((core * KVL + kvl) * GROUP + g) * HD, HD), HD)]

    def out_local(kvl, g):
        return pltpu.make_async_copy(
            obuf.at[kvl, g, pl.ds(row0, ROWS), :], out_cols(c, kvl, g), olocal.at[kvl, g]
        )

    def out_remote(kvl, g):
        return remote(
            obuf.at[kvl, g, pl.ds(row1, ROWS), :], out_cols(c, kvl, g), osend.at[kvl, g], orecv.at[kvl, g], partner
        )

    def attend_and_send(kvl, g):
        attend(kvl, g)
        out_local(kvl, g).start()
        out_remote(kvl, g).start()

    stage0(jnp.int32(0))

    def slot(n, carry):
        def when(t, what, low=0, high=CHUNKS):
            @pl.when((t >= low) & (t < high))
            def _():
                what(t)

        when(n + 1, stage0)

        @pl.when(n == 0)
        def _():
            normalise()

        when(n, stage1)

        @pl.when(n == 0)
        def _():
            rotate_queries()

        def z1(t):
            z_wait(t, 0)
            z_send(t, 1)

        def z2(t):
            z_wait(t, 1)
            z_send(t, 2)

        def z3(t):
            z_wait(t, 2)
            z_send(t, 3)

        def unit(which):
            u = 2 * (n - 6) + which

            @pl.when((u >= 0) & (u < KVL * GROUP))
            def _():
                attend_and_send(lax.div(u, GROUP), lax.rem(u, GROUP))

        when(n - 4, z1)
        when(n - 1, stage2)
        when(n - 5, lambda t: z_wait(t, 3))
        unit(0)
        when(n - 4, z2)

        @pl.when(n == 1)
        def _():
            make_bias()

        when(n - 2, stage3)
        unit(1)
        when(n - 4, z3)

        @pl.when(n == 2)
        def _():
            remote(nrm_landing, nrm_landing, core_send.at[0], core_recv.at[0], partner).wait_recv()
            remote(q_landing, q_landing, core_send.at[1], core_recv.at[1], partner).wait_recv()

        def compute(t):
            stage4(t)
            project(t)
            z_send(t, 0)

        when(n - 3, compute)
        return carry

    lax.fori_loop(0, 14, slot, 0)

    nrm_copy.wait_send()
    q_rot_copy.wait_send()

    @pl.loop(0, CHUNKS)
    def _(t):
        sent = nrm.at[:, pl.ds(0, 15 * HD)]
        pltpu.make_async_copy(sent, sent, wsend.at[t]).wait()
        around = kv.at[t, pl.ds(0, 7)]
        pltpu.make_async_copy(around, around, zsend.at[t]).wait()

    @pl.loop(0, KVL * GROUP)
    def _(u):
        kvl, g = lax.div(u, GROUP), lax.rem(u, GROUP)
        out_local(kvl, g).wait()
        out_remote(kvl, g).wait_send()
        theirs = out_cols(1 - c, kvl, g)
        remote(theirs, theirs, osend.at[kvl, g], orecv.at[kvl, g], partner).wait_recv()


def on_device(tokens, queries, norm_gain, w_key, w_value, block_list):
    s = lax.axis_index("seq")
    c, z = lax.rem(s, 2), lax.div(s, 2)
    heads = KVL * GROUP
    lists = lax.dynamic_slice(block_list[0], (c * heads, z * QB, 0), (heads, QB, block_list.shape[3]))
    lists = lists.reshape(heads * QB, block_list.shape[3])
    cosine, sine = rotary_tables()
    bf16, f32 = jnp.bfloat16, jnp.float32
    dma = pltpu.SemaphoreType.DMA
    out = pl.pallas_call(
        kernel,
        name="layer",
        out_shape=jax.ShapeDtypeStruct((ROWS, D), bf16),
        in_specs=[pl.BlockSpec(memory_space=pl.ANY)] * 8,
        out_specs=pl.BlockSpec(memory_space=pl.ANY),
        scratch_shapes=[
            pltpu.VMEM((CHUNKS, NX, NY, 2, 128, HD), bf16),
            pltpu.VMEM((PAIR, D), bf16),
            pltpu.VMEM((ROWS, D), bf16),
            pltpu.VMEM((1, D), f32),
            pltpu.VMEM((ROWS, D), bf16),
            pltpu.VMEM((KVL, GROUP, PAIR, HD), bf16),
            pltpu.VMEM((KVL, GROUP, ROWS, HD), bf16),
            pltpu.VMEM((CHUNKS, NZ, PAIR, HD), bf16),
            pltpu.VMEM((2, PAIR, HD), f32),
            pltpu.VMEM((2, PAIR, HD), f32),
            pltpu.VMEM((heads * QB, block_list.shape[3]), jnp.int32),
            pltpu.VMEM((heads * QB, LENGTH), f32),
            pltpu.VMEM((PAIR, PAIR), f32),
            pltpu.VMEM((PAIR, LENGTH), f32),
            pltpu.VMEM((KVL, GROUP, PAIR, HD), bf16),
            dma((6,)),
            dma((CHUNKS,)),
            dma((CHUNKS,)),
            dma((CHUNKS, 4, 2, 2)),
            dma((CHUNKS,)),
            dma((CHUNKS, 4, 2)),
            dma((2,)),
            dma((2,)),
            dma((KVL, GROUP)),
            dma((KVL, GROUP)),
            dma((KVL, GROUP)),
        ],
        compiler_params=pltpu.CompilerParams(
            collective_id=0, has_side_effects=True, vmem_limit_bytes=56 * 2**20
        ),
        cost_estimate=pl.CostEstimate(
            flops=6_400_000_000, bytes_accessed=6_000_000, transcendentals=8_400_000
        ),
    )(
        tokens[0],
        queries[0],
        norm_gain[None],
        w_key.reshape(2, 128, w_key.shape[1]),
        w_value.reshape(2, 128, w_value.shape[1]),
        lists,
        jnp.asarray(cosine),
        jnp.asarray(sine),
    )
    return out[None]


def solution(mesh):
    in_specs = (
        P("fsdp", "seq", None),
        P("fsdp", "seq", None),
        P(),
        P("fsdp", None),
        P("fsdp", None),
        P("fsdp", None, None, None),
    )
    return jax.shard_map(
        on_device, mesh=mesh, in_specs=in_specs, out_specs=P("fsdp", "seq", None), check_vma=False
    )
```

```python
import functools
import math

import jax
import jax.numpy as jnp
import numpy as np
from jax import lax
from jax.experimental import pallas as pl
from jax.experimental.pallas import tpu as pltpu
from jax.sharding import PartitionSpec as P

MESH = pl.DeviceIdType.MESH
EPS = 1e-05
ROPE_BASE = 500000.0
D = 4096
HD = 128
LENGTH = 2048
NX, NY, NZ = 4, 4, 8
KVL = 4
GROUP = 4
CHUNKS = 2 * KVL
ROWS = 128
PAIR = 2 * ROWS
BLOCK = 64
QB = PAIR // BLOCK
PLACES = 16
NQB = LENGTH // BLOCK
HIDDEN = -1e30
SCALE = math.log2(math.e) / math.sqrt(HD)


def rotary_tables():
    freqs = np.float32(ROPE_BASE) ** (
        -np.arange(HD // 2, dtype=np.float32) * np.float32(2.0 / HD)
    )
    angles = np.arange(LENGTH, dtype=np.float32)[:, None] * freqs.astype(np.float32)[None, :]
    cosine = np.cos(angles.astype(np.float64)).astype(np.float32)
    sine = np.sin(angles.astype(np.float64)).astype(np.float32)
    return np.concatenate([cosine, cosine], 1), np.concatenate([-sine, sine], 1)


def kernel(
    tokens, queries, gain, wk, wv, lists, cos_hbm, sin_hbm, out,
    wbuf, nrm, tok, gn, qin, qrot, qsend, kv, cs, sn, lst, qmask, spread, tri, sbuf, mbuf, pbuf, tbuf, abuf, obuf,
    in_sem, own_sem, wsend, wrecv, zsend, zrecv, core_send, core_recv, osend, orecv,
):
    s = lax.axis_index("seq")
    f = lax.axis_index("fsdp")
    c = lax.rem(s, 2)
    z = lax.div(s, 2)
    x = lax.div(f, NY)
    y = lax.rem(f, NY)
    xn, xp = lax.rem(x + NX - 1, NX), lax.rem(x + 1, NX)
    yn, yp = lax.rem(y + NY - 1, NY), lax.rem(y + 1, NY)
    x2, y2 = lax.rem(x + 2, NX), lax.rem(y + 2, NY)
    x_dev = ((s, xp * NY + y), (s, xn * NY + y))
    y_dev = ((s, x * NY + yp), (s, x * NY + yn))
    z_dev = ((lax.rem(s + 2, 2 * NZ), f), (lax.rem(s + 2 * NZ - 2, 2 * NZ), f))
    partner = (s + 1 - 2 * c, f)
    row0 = pl.multiple_of(c * ROWS, ROWS)
    row1 = pl.multiple_of((1 - c) * ROWS, ROWS)

    def own_copy(t):
        kvl = lax.div(t, 2)
        cols = pl.ds(pl.multiple_of((KVL * c + kvl) * HD, HD), HD)
        return [
            pltpu.make_async_copy(w.at[:, :, cols], wbuf.at[t, x, y], own_sem.at[t])
            for w in (wk, wv)
        ]

    def start_own(t):
        key_copy, value_copy = own_copy(t)

        @pl.when(lax.rem(t, 2) == 0)
        def _():
            key_copy.start()

        @pl.when(lax.rem(t, 2) == 1)
        def _():
            value_copy.start()

    pos = pl.ds(pl.multiple_of(z * PAIR, PAIR), PAIR)
    tok_copy = pltpu.make_async_copy(tokens, tok, in_sem.at[0])
    gain_copy = pltpu.make_async_copy(gain, gn, in_sem.at[1])
    q_copy = pltpu.make_async_copy(queries, qin, in_sem.at[2])
    cos_copy = pltpu.make_async_copy(cos_hbm.at[pos, :], cs.at[0], in_sem.at[3])
    sin_copy = pltpu.make_async_copy(sin_hbm.at[pos, :], sn.at[0], in_sem.at[4])
    list_copy = pltpu.make_async_copy(
        lists.at[pl.ds(c * KVL * GROUP, KVL * GROUP)], lst, in_sem.at[5]
    )

    start_own(0)
    start_own(1)
    tok_copy.start()
    gain_copy.start()
    cos_copy.start()
    sin_copy.start()
    q_copy.start()
    list_copy.start()
    for t in range(2, CHUNKS):
        start_own(t)

    barrier = pltpu.get_barrier_semaphore()
    for device in (*x_dev, *y_dev, *z_dev, partner):
        pl.semaphore_signal(barrier, inc=1, device_id=device, device_id_type=MESH)
    pl.semaphore_wait(barrier, 7)

    def remote(src, dst, send, recv, device):
        return pltpu.make_async_remote_copy(
            src_ref=src, dst_ref=dst, send_sem=send, recv_sem=recv, device_id=device, device_id_type=MESH
        )

    first_dev = (x_dev, y_dev)
    second_dev = (y_dev, x_dev)

    def piece(t, half, step):
        if half == 0:
            return wbuf.at[t, (x, xn, x2, xp)[step], y, 0]
        return wbuf.at[t, x, (y, yn, y2, yp)[step], 1]

    def line(t, half, step, part):
        some = pl.ds(2 * part, 2)
        if half == 0:
            return wbuf.at[t, some, (y, yn, y2, yp)[step], 0]
        return wbuf.at[t, (x, xn, x2, xp)[step], some, 1]

    def rows_of(ref, part):
        return ref.at[pl.ds(64 * part, 64), :]

    def w_send(t, stage, half, d, ref, device):
        remote(ref, ref, wsend.at[t], wrecv.at[t, stage, half, d], device).start()

    def w_wait(t, stage, half, d, ref):
        remote(ref, ref, wsend.at[t], wrecv.at[t, stage, half, d], partner).wait_recv()

    def stage0(t):
        own_copy(t)[0].wait()
        for half in range(2):
            for d in range(2):
                w_send(t, 0, half, d, piece(t, half, 0), first_dev[half][d])

    def stage1(t):
        for half in range(2):
            for d, step in ((0, 1), (1, 3)):
                w_wait(t, 0, half, d, piece(t, half, step))
                w_send(t, 1, half, d, rows_of(piece(t, half, step), d), first_dev[half][d])

    def stage2(t):
        for half in range(2):
            for d in range(2):
                w_wait(t, 1, half, d, rows_of(piece(t, half, 2), d))
            for d in range(2):
                w_send(t, 2, half, d, line(t, half, 0, d), second_dev[half][d])
        for half in range(2):
            for d in range(2):
                w_send(t, 3, half, d, line(t, half, 0, 1 - d), second_dev[half][d])

    def stage3(t):
        for half in range(2):
            for d, step in ((0, 1), (1, 3)):
                w_wait(t, 2, half, d, line(t, half, step, d))
                w_send(t, 4, half, d, line(t, half, step, d), second_dev[half][d])

    def stage4(t):
        for half in range(2):
            for d, step in ((0, 1), (1, 3)):
                w_wait(t, 3, half, d, line(t, half, step, 1 - d))
                w_wait(t, 4, half, d, line(t, half, 2, d))

    def z_slot(t, stage, d):
        if stage == 3:
            return kv.at[t, 4, pl.ds(128 * d, 128), :]
        return kv.at[t, stage + 1 if d == 0 else 7 - stage]

    def z_source(t, stage, d):
        if stage == 3:
            return kv.at[t, 3 if d == 0 else 5, pl.ds(128 * d, 128), :]
        return kv.at[t, stage if d == 0 else (8 - stage) % 8]

    def z_send(t, stage):
        for d in range(2):
            remote(
                z_source(t, stage, d), z_slot(t, stage, d), zsend.at[t], zrecv.at[t, stage, d], z_dev[d]
            ).start()

    def z_wait(t, stage):
        for d in range(2):
            ref = z_slot(t, stage, d)
            remote(ref, ref, zsend.at[t], zrecv.at[t, stage, d], partner).wait_recv()

    nrm_copy = remote(
        nrm.at[pl.ds(row0, ROWS), :], nrm.at[pl.ds(row0, ROWS), :], core_send.at[0], core_recv.at[0], partner
    )
    q_rot_copy = remote(
        qsend, qrot.at[:, :, pl.ds(row0, ROWS), :], core_send.at[1], core_recv.at[1], partner
    )
    nrm_landing = nrm.at[pl.ds(row1, ROWS), :]
    q_landing = qrot.at[:, :, pl.ds(row1, ROWS), :]

    def normalise():
        tok_copy.wait()
        gain_copy.wait()

        @pl.loop(0, ROWS // 16)
        def _(i):
            rows = pl.ds(pl.multiple_of(i * 16, 16), 16)
            wide = tok[rows, :].astype(jnp.float32)
            mean = jnp.sum(wide * wide, axis=-1, keepdims=True) * (1.0 / D)
            normed = wide * lax.rsqrt(mean + EPS) * gn[...]
            nrm[pl.ds(pl.multiple_of(row0 + i * 16, 16), 16), :] = normed.astype(jnp.bfloat16)

        nrm_copy.start()

    def rotate_queries():
        q_copy.wait()
        cos_copy.wait()
        sin_copy.wait()
        cs[1] = jnp.ones((PAIR, HD), jnp.float32)
        sn[1] = jnp.zeros((PAIR, HD), jnp.float32)

        def rotated(head):
            cols = pl.ds(pl.multiple_of(head * HD, HD), HD)
            v = qin[:, cols].astype(jnp.float32)
            turned = v * cs[0, pl.ds(row0, ROWS), :] + pltpu.roll(v, HD // 2, 1) * sn[0, pl.ds(row0, ROWS), :]
            return turned.astype(jnp.bfloat16)

        @pl.loop(0, KVL * GROUP)
        def _(h):
            kvl, g = lax.div(h, GROUP), lax.rem(h, GROUP)
            qsend[kvl, g] = rotated((1 - c) * KVL * GROUP + h)
            qrot[kvl, g, pl.ds(row0, ROWS), :] = rotated(c * KVL * GROUP + h)

        q_rot_copy.start()

    def make_masks():
        list_copy.wait()
        shape = (8, NQB)
        row, lane = (lax.broadcasted_iota(jnp.int32, shape, d) for d in (0, 1))
        mine = (lane == z * QB + row).astype(jnp.bfloat16)
        ids = lst[...].reshape(KVL * GROUP * PLACES, NQB).astype(jnp.float32).astype(jnp.bfloat16)
        picked = lax.dot_general(mine, ids, (((1,), (1,)), ((), ())), preferred_element_type=jnp.float32)
        number = lax.broadcasted_iota(jnp.int32, (8, HD), 1).astype(jnp.float32)
        for h in range(KVL * GROUP):
            hit = picked[:, h * PLACES : h * PLACES + 1] == number
            for place in range(1, PLACES):
                at = h * PLACES + place
                hit = hit | (picked[:, at : at + 1] == number)
            hide = jnp.where(hit, 0.0, HIDDEN)
            for b in range(QB):
                qmask[h, b * BLOCK : (b + 1) * BLOCK, :] = jnp.broadcast_to(
                    hide[b : b + 1, :], (BLOCK, HD)
                ).astype(jnp.bfloat16)
        i = lax.broadcasted_iota(jnp.int32, (PAIR, HD), 0)
        j = lax.broadcasted_iota(jnp.int32, (PAIR, HD), 1)
        for r in range(NZ):
            block = lax.rem(z - r + NZ, NZ) * QB + lax.div(i, BLOCK)
            spread[r] = (block == j).astype(jnp.float32).astype(jnp.bfloat16)
        i = lax.broadcasted_iota(jnp.int32, (PAIR, PAIR), 0)
        j = lax.broadcasted_iota(jnp.int32, (PAIR, PAIR), 1)
        tri[...] = jnp.where(j <= i, 0.0, HIDDEN)

    def project(t):
        acc = jnp.dot(nrm[...], wbuf[t].reshape(D, HD), preferred_element_type=jnp.float32)
        kind = lax.rem(t, 2)
        kv[t, 0] = (acc * cs[kind] + pltpu.roll(acc, HD // 2, 1) * sn[kind]).astype(jnp.bfloat16)

    def score(u, at):
        kvl, g = lax.div(u, GROUP), lax.rem(u, GROUP)
        q = jnp.concatenate([qrot[kvl, g], qmask[u]], 1)
        top = None
        for r in range(NZ):
            keys = jnp.concatenate([kv[2 * kvl, r], spread[r]], 1)
            scores = lax.dot_general(q, keys, (((1,), (1,)), ((), ())), preferred_element_type=jnp.float32)
            if r == 0:
                scores = scores + tri[...]
            sbuf[at, :, r * PAIR : (r + 1) * PAIR] = scores
            here = jnp.maximum(scores[:, :HD], scores[:, HD:])
            top = here if top is None else jnp.maximum(top, here)
        mbuf[at] = jnp.broadcast_to(jnp.max(top, axis=-1, keepdims=True), (PAIR, HD))

    def soften(u, at):
        g = lax.rem(u, GROUP)
        top, total = mbuf[at], None
        for r in range(LENGTH // HD):
            cols = slice(r * HD, (r + 1) * HD)
            p = jnp.exp2((sbuf[at, :, cols] - top) * SCALE)
            total = p if total is None else total + p
            pbuf[g, :, cols] = p.astype(jnp.bfloat16)
        tbuf[g] = jnp.broadcast_to(jnp.sum(total, axis=-1, keepdims=True), (PAIR, HD))

    def weigh(u):
        kvl, g = lax.div(u, GROUP), lax.rem(u, GROUP)
        values = kv[2 * kvl + 1].reshape(LENGTH, HD)
        acc = jnp.dot(pbuf[g], values, preferred_element_type=jnp.float32)
        abuf[g] = acc / tbuf[g]
        obuf[kvl, g] = abuf[g, pl.ds(row1, ROWS), :].astype(jnp.bfloat16)
        cols = pl.ds(pl.multiple_of((c * KVL * GROUP + u) * HD, HD), HD)
        out[:, cols] = abuf[g, pl.ds(row0, ROWS), :].astype(jnp.bfloat16)

    def out_cols(core, kvl, g):
        return out.at[:, pl.ds(pl.multiple_of(((core * KVL + kvl) * GROUP + g) * HD, HD), HD)]

    def out_remote(kvl, g):
        return remote(
            obuf.at[kvl, g], out_cols(c, kvl, g), osend.at[kvl, g], orecv.at[kvl, g], partner
        )

    def pair_scores(m):
        for i in range(2):
            score(2 * m + i, i)
        for i in range(2):
            soften(2 * m + i, i)

    def pair_values(m):
        for i in range(2):
            weigh(2 * m + i)
        for i in range(2):
            u = 2 * m + i
            out_remote(lax.div(u, GROUP), lax.rem(u, GROUP)).start()

    def around(stage):
        def step(t):
            z_wait(t, stage - 1)
            if stage < 4:
                z_send(t, stage)

        return step

    def compute(t):
        stage4(t)

        @pl.when(t == 0)
        def _():
            remote(nrm_landing, nrm_landing, core_send.at[0], core_recv.at[0], partner).wait_recv()

        project(t)
        z_send(t, 0)

    for t in range(4):
        stage0(t)
    normalise()
    for t in range(2):
        stage1(t)

    def slot(n, carry):
        def when(t, what, low=0, high=CHUNKS):
            @pl.when((t >= low) & (t < high))
            def _():
                what(t)

        when(n + 4, stage0)
        when(n - 1, stage3)
        when(n + 2, stage1, 2)
        when(n - 6, pair_values)
        when(n - 3, around(2))
        when(n, stage2)

        @pl.when(n == 0)
        def _():
            rotate_queries()

        @pl.when(n == 1)
        def _():
            make_masks()

        @pl.when(n == 5)
        def _():
            remote(q_landing, q_landing, core_send.at[1], core_recv.at[1], partner).wait_recv()

        when(n - 5, pair_scores)
        when(n - 2, around(1))
        when(n - 1, compute)
        when(n - 4, around(4))
        when(n - 3, around(3))
        return carry

    lax.fori_loop(0, 11, slot, 0)

    pair_values(5)
    pair_scores(6)
    pair_scores(7)
    around(4)(7)
    pair_values(6)
    pair_values(7)

    nrm_copy.wait_send()
    q_rot_copy.wait_send()

    @pl.loop(0, CHUNKS)
    def _(t):
        sent = nrm.at[:, pl.ds(0, 15 * HD)]
        pltpu.make_async_copy(sent, sent, wsend.at[t]).wait()
        around = kv.at[t, pl.ds(0, 7)]
        pltpu.make_async_copy(around, around, zsend.at[t]).wait()

    @pl.loop(0, KVL * GROUP)
    def _(u):
        kvl, g = lax.div(u, GROUP), lax.rem(u, GROUP)
        out_remote(kvl, g).wait_send()
        theirs = out_cols(1 - c, kvl, g)
        remote(theirs, theirs, osend.at[kvl, g], orecv.at[kvl, g], partner).wait_recv()


def on_device(tokens, queries, norm_gain, w_key, w_value, block_list):
    heads = KVL * GROUP
    cosine, sine = rotary_tables()
    bf16, f32 = jnp.bfloat16, jnp.float32
    dma = pltpu.SemaphoreType.DMA
    out = pl.pallas_call(
        kernel,
        name="layer",
        out_shape=pltpu.VMEM((ROWS, D), bf16),
        in_specs=[pl.BlockSpec(memory_space=pl.ANY)] * 8,
        out_specs=pl.BlockSpec(memory_space=pltpu.VMEM),
        scratch_shapes=[
            pltpu.VMEM((CHUNKS, NX, NY, 2, 128, HD), bf16),
            pltpu.VMEM((PAIR, D), bf16),
            pltpu.VMEM((ROWS, D), bf16),
            pltpu.VMEM((1, D), f32),
            pltpu.VMEM((ROWS, D), bf16),
            pltpu.VMEM((KVL, GROUP, PAIR, HD), bf16),
            pltpu.VMEM((KVL, GROUP, ROWS, HD), bf16),
            pltpu.VMEM((CHUNKS, NZ, PAIR, HD), bf16),
            pltpu.VMEM((2, PAIR, HD), f32),
            pltpu.VMEM((2, PAIR, HD), f32),
            pltpu.VMEM((heads, PLACES, NQB), jnp.int32),
            pltpu.VMEM((heads, PAIR, HD), bf16),
            pltpu.VMEM((NZ, PAIR, HD), bf16),
            pltpu.VMEM((PAIR, PAIR), f32),
            pltpu.VMEM((2, PAIR, LENGTH), f32),
            pltpu.VMEM((2, PAIR, HD), f32),
            pltpu.VMEM((GROUP, PAIR, LENGTH), bf16),
            pltpu.VMEM((GROUP, PAIR, HD), f32),
            pltpu.VMEM((GROUP, PAIR, HD), f32),
            pltpu.VMEM((KVL, GROUP, ROWS, HD), bf16),
            dma((6,)),
            dma((CHUNKS,)),
            dma((CHUNKS,)),
            dma((CHUNKS, 5, 2, 2)),
            dma((CHUNKS,)),
            dma((CHUNKS, 4, 2)),
            dma((2,)),
            dma((2,)),
            dma((KVL, GROUP)),
            dma((KVL, GROUP)),
        ],
        compiler_params=pltpu.CompilerParams(
            collective_id=0, has_side_effects=True, vmem_limit_bytes=56 * 2**20
        ),
        cost_estimate=pl.CostEstimate(
            flops=6_400_000_000, bytes_accessed=6_000_000, transcendentals=8_400_000
        ),
    )(
        tokens[0],
        queries[0],
        norm_gain[None],
        w_key.reshape(2, 128, w_key.shape[1]),
        w_value.reshape(2, 128, w_value.shape[1]),
        block_list[0].transpose(0, 2, 1),
        jnp.asarray(cosine),
        jnp.asarray(sine),
    )
    return out[None]


def solution(mesh):
    in_specs = (
        P("fsdp", "seq", None),
        P("fsdp", "seq", None),
        P(),
        P("fsdp", None),
        P("fsdp", None),
        P("fsdp", None, None, None),
    )
    return jax.shard_map(
        on_device, mesh=mesh, in_specs=in_specs, out_specs=P("fsdp", "seq", None), check_vma=False
    )
```

```python
import functools
import math

import jax
import jax.numpy as jnp
import numpy as np
from jax import lax
from jax.experimental import pallas as pl
from jax.experimental.pallas import tpu as pltpu
from jax.sharding import PartitionSpec as P

MESH = pl.DeviceIdType.MESH
EPS = 1e-05
ROPE_BASE = 500000.0
D = 4096
HD = 128
LENGTH = 2048
NX, NY, NZ = 4, 4, 8
KVL = 4
GROUP = 4
CHUNKS = 2 * KVL
ROWS = 128
PAIR = 2 * ROWS
BLOCK = 64
QB = PAIR // BLOCK
PLACES = 16
NQB = LENGTH // BLOCK
HIDDEN = -1e30
SCALE = math.log2(math.e) / math.sqrt(HD)


def rotary_tables():
    freqs = np.float32(ROPE_BASE) ** (
        -np.arange(HD // 2, dtype=np.float32) * np.float32(2.0 / HD)
    )
    angles = np.arange(LENGTH, dtype=np.float32)[:, None] * freqs.astype(np.float32)[None, :]
    cosine = np.cos(angles.astype(np.float64)).astype(np.float32)
    sine = np.sin(angles.astype(np.float64)).astype(np.float32)
    return np.concatenate([cosine, cosine], 1), np.concatenate([-sine, sine], 1)


def kernel(
    tokens, queries, gain, wk, wv, lists, cos_hbm, sin_hbm, out,
    wbuf, nrm, tok, gn, qin, qrot, qsend, kv, cs, sn, lst, qmask, spread, tri, sbuf, mbuf, pbuf, tbuf, abuf, obuf,
    in_sem, own_sem, wsend, wrecv, zsend, zrecv, core_send, core_recv, osend, orecv,
):
    s = lax.axis_index("seq")
    f = lax.axis_index("fsdp")
    c = lax.rem(s, 2)
    z = lax.div(s, 2)
    x = lax.div(f, NY)
    y = lax.rem(f, NY)
    xn, xp = lax.rem(x + NX - 1, NX), lax.rem(x + 1, NX)
    yn, yp = lax.rem(y + NY - 1, NY), lax.rem(y + 1, NY)
    x2, y2 = lax.rem(x + 2, NX), lax.rem(y + 2, NY)
    x_dev = ((s, xp * NY + y), (s, xn * NY + y))
    y_dev = ((s, x * NY + yp), (s, x * NY + yn))
    z_dev = ((lax.rem(s + 2, 2 * NZ), f), (lax.rem(s + 2 * NZ - 2, 2 * NZ), f))
    partner = (s + 1 - 2 * c, f)
    row0 = pl.multiple_of(c * ROWS, ROWS)
    row1 = pl.multiple_of((1 - c) * ROWS, ROWS)

    def own_copy(t):
        kvl = lax.div(t, 2)
        cols = pl.ds(pl.multiple_of((KVL * c + kvl) * HD, HD), HD)
        return [
            pltpu.make_async_copy(w.at[:, :, cols], wbuf.at[t, x, y], own_sem.at[t])
            for w in (wk, wv)
        ]

    def start_own(t):
        key_copy, value_copy = own_copy(t)

        @pl.when(lax.rem(t, 2) == 0)
        def _():
            key_copy.start()

        @pl.when(lax.rem(t, 2) == 1)
        def _():
            value_copy.start()

    pos = pl.ds(pl.multiple_of(z * PAIR, PAIR), PAIR)
    tok_copy = pltpu.make_async_copy(tokens, tok, in_sem.at[0])
    gain_copy = pltpu.make_async_copy(gain, gn, in_sem.at[1])
    q_copy = pltpu.make_async_copy(queries, qin, in_sem.at[2])
    cos_copy = pltpu.make_async_copy(cos_hbm.at[pos, :], cs.at[0], in_sem.at[3])
    sin_copy = pltpu.make_async_copy(sin_hbm.at[pos, :], sn.at[0], in_sem.at[4])
    list_copy = pltpu.make_async_copy(
        lists.at[pl.ds(c * KVL * GROUP, KVL * GROUP)], lst, in_sem.at[5]
    )

    start_own(0)
    start_own(1)
    tok_copy.start()
    gain_copy.start()
    cos_copy.start()
    sin_copy.start()
    q_copy.start()
    list_copy.start()
    for t in range(2, CHUNKS):
        start_own(t)

    barrier = pltpu.get_barrier_semaphore()
    for device in (*x_dev, *y_dev, *z_dev, partner):
        pl.semaphore_signal(barrier, inc=1, device_id=device, device_id_type=MESH)
    pl.semaphore_wait(barrier, 7)

    def remote(src, dst, send, recv, device):
        return pltpu.make_async_remote_copy(
            src_ref=src, dst_ref=dst, send_sem=send, recv_sem=recv, device_id=device, device_id_type=MESH
        )

    first_dev = (x_dev, y_dev)
    second_dev = (y_dev, x_dev)

    def piece(t, half, step):
        if half == 0:
            return wbuf.at[t, (x, xn, x2, xp)[step], y, 0]
        return wbuf.at[t, x, (y, yn, y2, yp)[step], 1]

    def line(t, half, step, part):
        some = pl.ds(2 * part, 2)
        if half == 0:
            return wbuf.at[t, some, (y, yn, y2, yp)[step], 0]
        return wbuf.at[t, (x, xn, x2, xp)[step], some, 1]

    def rows_of(ref, part):
        return ref.at[pl.ds(64 * part, 64), :]

    def w_send(t, stage, half, d, ref, device):
        remote(ref, ref, wsend.at[t], wrecv.at[t, stage, half, d], device).start()

    def w_wait(t, stage, half, d, ref):
        remote(ref, ref, wsend.at[t], wrecv.at[t, stage, half, d], partner).wait_recv()

    def stage0(t):
        own_copy(t)[0].wait()
        for half in range(2):
            for d in range(2):
                w_send(t, 0, half, d, piece(t, half, 0), first_dev[half][d])

    def stage1(t):
        for half in range(2):
            for d, step in ((0, 1), (1, 3)):
                w_wait(t, 0, half, d, piece(t, half, step))
                w_send(t, 1, half, d, rows_of(piece(t, half, step), d), first_dev[half][d])

    def stage2(t):
        for half in range(2):
            for d in range(2):
                w_wait(t, 1, half, d, rows_of(piece(t, half, 2), d))
            for d in range(2):
                w_send(t, 2, half, d, line(t, half, 0, d), second_dev[half][d])
        for half in range(2):
            for d in range(2):
                w_send(t, 3, half, d, line(t, half, 0, 1 - d), second_dev[half][d])

    def stage3(t):
        for half in range(2):
            for d, step in ((0, 1), (1, 3)):
                w_wait(t, 2, half, d, line(t, half, step, d))
                w_send(t, 4, half, d, line(t, half, step, d), second_dev[half][d])

    def stage4(t):
        for half in range(2):
            for d, step in ((0, 1), (1, 3)):
                w_wait(t, 3, half, d, line(t, half, step, 1 - d))
                w_wait(t, 4, half, d, line(t, half, 2, d))

    def z_slot(t, stage, d):
        if stage == 3:
            return kv.at[t, 4, pl.ds(128 * d, 128), :]
        return kv.at[t, stage + 1 if d == 0 else 7 - stage]

    def z_source(t, stage, d):
        if stage == 3:
            return kv.at[t, 3 if d == 0 else 5, pl.ds(128 * d, 128), :]
        return kv.at[t, stage if d == 0 else (8 - stage) % 8]

    def arrives(stage, d, chip):
        if d == 0:
            return chip >= stage + 1
        return (chip + stage + 1 < NZ // 2) | (chip + stage + 1 >= NZ)

    def leaves(stage, d):
        if d == 0:
            return (z < NZ - 1) & (z >= stage)
        return arrives(stage, d, lax.rem(z + NZ - 1, NZ))

    def z_send(t, stage):
        for d in range(2):

            @pl.when(leaves(stage, d))
            def _():
                remote(
                    z_source(t, stage, d), z_slot(t, stage, d), zsend.at[t], zrecv.at[t, stage, d], z_dev[d]
                ).start()

    def z_wait(t, stage):
        for d in range(2):

            @pl.when(arrives(stage, d, z))
            def _():
                ref = z_slot(t, stage, d)
                remote(ref, ref, zsend.at[t], zrecv.at[t, stage, d], partner).wait_recv()

    def z_sent(t):
        refs = {
            5: wbuf.at[pl.ds(0, 5), 0, 0, 0],
            7: wbuf.at[pl.ds(0, 7), 0, 0, 0],
            8: wbuf.at[pl.ds(0, 8), 0, 0, 0],
            9: qsend.at[pl.ds(0, 3), pl.ds(0, 3)],
            10: spread.at[pl.ds(0, 5)],
        }
        for units, chips in ((5, (7,)), (7, (4,)), (8, (5,)), (9, (0, 3)), (10, (1, 2, 6))):
            here = functools.reduce(jnp.logical_or, [z == chip for chip in chips])

            @pl.when(here)
            def _():
                pltpu.make_async_copy(refs[units], refs[units], zsend.at[t]).wait()

    def clear_rest():
        for r in range(1, NZ):
            used = arrives(r - 1, 0, z) if r <= NZ // 2 else arrives(NZ - 1 - r, 1, z)

            @pl.when(jnp.logical_not(used))
            def _():
                @pl.loop(0, CHUNKS)
                def _(t):
                    kv[t, r] = jnp.zeros((PAIR, HD), jnp.bfloat16)

    nrm_copy = remote(
        nrm.at[pl.ds(row0, ROWS), :], nrm.at[pl.ds(row0, ROWS), :], core_send.at[0], core_recv.at[0], partner
    )
    q_rot_copy = remote(
        qsend, qrot.at[:, :, pl.ds(row0, ROWS), :], core_send.at[1], core_recv.at[1], partner
    )
    nrm_landing = nrm.at[pl.ds(row1, ROWS), :]
    q_landing = qrot.at[:, :, pl.ds(row1, ROWS), :]

    def normalise():
        tok_copy.wait()
        gain_copy.wait()

        @pl.loop(0, ROWS // 16)
        def _(i):
            rows = pl.ds(pl.multiple_of(i * 16, 16), 16)
            wide = tok[rows, :].astype(jnp.float32)
            mean = jnp.sum(wide * wide, axis=-1, keepdims=True) * (1.0 / D)
            normed = wide * lax.rsqrt(mean + EPS) * gn[...]
            nrm[pl.ds(pl.multiple_of(row0 + i * 16, 16), 16), :] = normed.astype(jnp.bfloat16)

        nrm_copy.start()

    def rotate_queries():
        q_copy.wait()
        cos_copy.wait()
        sin_copy.wait()
        cs[1] = jnp.ones((PAIR, HD), jnp.float32)
        sn[1] = jnp.zeros((PAIR, HD), jnp.float32)

        def rotated(head):
            cols = pl.ds(pl.multiple_of(head * HD, HD), HD)
            v = qin[:, cols].astype(jnp.float32)
            turned = v * cs[0, pl.ds(row0, ROWS), :] + pltpu.roll(v, HD // 2, 1) * sn[0, pl.ds(row0, ROWS), :]
            return turned.astype(jnp.bfloat16)

        @pl.loop(0, KVL * GROUP)
        def _(h):
            kvl, g = lax.div(h, GROUP), lax.rem(h, GROUP)
            qsend[kvl, g] = rotated((1 - c) * KVL * GROUP + h)
            qrot[kvl, g, pl.ds(row0, ROWS), :] = rotated(c * KVL * GROUP + h)

        q_rot_copy.start()

    def make_masks():
        list_copy.wait()
        shape = (8, NQB)
        row, lane = (lax.broadcasted_iota(jnp.int32, shape, d) for d in (0, 1))
        mine = (lane == z * QB + row).astype(jnp.bfloat16)
        ids = lst[...].reshape(KVL * GROUP * PLACES, NQB).astype(jnp.float32).astype(jnp.bfloat16)
        picked = lax.dot_general(mine, ids, (((1,), (1,)), ((), ())), preferred_element_type=jnp.float32)
        number = lax.broadcasted_iota(jnp.int32, (8, HD), 1).astype(jnp.float32)
        for h in range(KVL * GROUP):
            hit = picked[:, h * PLACES : h * PLACES + 1] == number
            for place in range(1, PLACES):
                at = h * PLACES + place
                hit = hit | (picked[:, at : at + 1] == number)
            hide = jnp.where(hit, 0.0, HIDDEN)
            for b in range(QB):
                qmask[h, b * BLOCK : (b + 1) * BLOCK, :] = jnp.broadcast_to(
                    hide[b : b + 1, :], (BLOCK, HD)
                ).astype(jnp.bfloat16)
        i = lax.broadcasted_iota(jnp.int32, (PAIR, HD), 0)
        j = lax.broadcasted_iota(jnp.int32, (PAIR, HD), 1)
        for r in range(NZ):
            block = lax.rem(z - r + NZ, NZ) * QB + lax.div(i, BLOCK)
            spread[r] = (block == j).astype(jnp.float32).astype(jnp.bfloat16)
        i = lax.broadcasted_iota(jnp.int32, (PAIR, PAIR), 0)
        j = lax.broadcasted_iota(jnp.int32, (PAIR, PAIR), 1)
        tri[...] = jnp.where(j <= i, 0.0, HIDDEN)

    def project(t):
        acc = jnp.dot(nrm[...], wbuf[t].reshape(D, HD), preferred_element_type=jnp.float32)
        kind = lax.rem(t, 2)
        kv[t, 0] = (acc * cs[kind] + pltpu.roll(acc, HD // 2, 1) * sn[kind]).astype(jnp.bfloat16)

    def score(u, at):
        kvl, g = lax.div(u, GROUP), lax.rem(u, GROUP)
        q = jnp.concatenate([qrot[kvl, g], qmask[u]], 1)
        top = None
        for r in range(NZ):
            keys = jnp.concatenate([kv[2 * kvl, r], spread[r]], 1)
            scores = lax.dot_general(q, keys, (((1,), (1,)), ((), ())), preferred_element_type=jnp.float32)
            if r == 0:
                scores = scores + tri[...]
            sbuf[at, :, r * PAIR : (r + 1) * PAIR] = scores
            here = jnp.maximum(scores[:, :HD], scores[:, HD:])
            top = here if top is None else jnp.maximum(top, here)
        mbuf[at] = jnp.broadcast_to(jnp.max(top, axis=-1, keepdims=True), (PAIR, HD))

    def soften(u, at):
        place = lax.rem(u, 2 * GROUP)
        top, total = mbuf[at], None
        for r in range(LENGTH // HD):
            cols = slice(r * HD, (r + 1) * HD)
            p = jnp.exp2((sbuf[at, :, cols] - top) * SCALE)
            total = p if total is None else total + p
            pbuf[place, :, cols] = p.astype(jnp.bfloat16)
        tbuf[place] = jnp.broadcast_to(jnp.sum(total, axis=-1, keepdims=True), (PAIR, HD))

    def weigh(u):
        kvl, g = lax.div(u, GROUP), lax.rem(u, GROUP)
        values = kv[2 * kvl + 1].reshape(LENGTH, HD)
        place = lax.rem(u, 2 * GROUP)
        acc = jnp.dot(pbuf[place], values, preferred_element_type=jnp.float32)
        abuf[g] = acc / tbuf[place]
        obuf[kvl, g] = abuf[g, pl.ds(row1, ROWS), :].astype(jnp.bfloat16)
        cols = pl.ds(pl.multiple_of((c * KVL * GROUP + u) * HD, HD), HD)
        out[:, cols] = abuf[g, pl.ds(row0, ROWS), :].astype(jnp.bfloat16)

    def out_cols(core, kvl, g):
        return out.at[:, pl.ds(pl.multiple_of(((core * KVL + kvl) * GROUP + g) * HD, HD), HD)]

    def out_remote(kvl, g):
        return remote(
            obuf.at[kvl, g], out_cols(c, kvl, g), osend.at[kvl, g], orecv.at[kvl, g], partner
        )

    def pair_scores(m):
        for i in range(2):
            score(2 * m + i, i)
        for i in range(2):
            soften(2 * m + i, i)

    def pair_values(m):
        for i in range(2):
            weigh(2 * m + i)
        for i in range(2):
            u = 2 * m + i
            out_remote(lax.div(u, GROUP), lax.rem(u, GROUP)).start()

    def around(stage):
        def step(t):
            z_wait(t, stage - 1)
            if stage < 4:
                z_send(t, stage)

        return step

    def compute(t):
        stage4(t)

        @pl.when(t == 0)
        def _():
            remote(nrm_landing, nrm_landing, core_send.at[0], core_recv.at[0], partner).wait_recv()

        project(t)
        z_send(t, 0)

    for t in range(6):
        stage0(t)
    normalise()
    for t in range(6):
        stage1(t)
    for t in range(2):
        stage2(t)

    def slot(n, carry):
        def when(t, what, low=0, high=CHUNKS):
            @pl.when((t >= low) & (t < high))
            def _():
                what(t)

        when(n + 6, stage0)
        when(n - 4, around(2))
        when(n, stage3)
        when(n - 5, around(3))
        when(n - 1, compute)
        when(n - 6, around(4))
        when(n + 2, stage2)

        @pl.when(n == 0)
        def _():
            rotate_queries()

        @pl.when(n == 1)
        def _():
            make_masks()
            clear_rest()

        @pl.when(n == 5)
        def _():
            remote(q_landing, q_landing, core_send.at[1], core_recv.at[1], partner).wait_recv()

        when(n - 6, pair_scores)
        when(n + 6, stage1)
        when(n - 2, around(1))
        return carry

    lax.fori_loop(0, 9, slot, 0)

    around(2)(5)
    pl.loop(0, 2)(pair_values)
    around(3)(4)
    around(4)(3)
    pair_scores(3)
    around(1)(7)
    pl.loop(2, 4)(pair_values)
    around(2)(6)
    around(3)(5)
    around(4)(4)
    pair_scores(4)
    around(2)(7)
    pair_scores(5)
    around(3)(6)
    around(4)(5)
    pl.loop(4, 6)(pair_values)
    around(3)(7)
    around(4)(6)
    pl.loop(6, 8)(pair_scores)
    around(4)(7)
    pl.loop(6, 8)(pair_values)

    nrm_copy.wait_send()
    q_rot_copy.wait_send()

    @pl.loop(0, CHUNKS)
    def _(t):
        sent = nrm.at[:, pl.ds(0, 15 * HD)]
        pltpu.make_async_copy(sent, sent, wsend.at[t]).wait()
        z_sent(t)

    @pl.loop(0, KVL * GROUP)
    def _(u):
        kvl, g = lax.div(u, GROUP), lax.rem(u, GROUP)
        out_remote(kvl, g).wait_send()
        theirs = out_cols(1 - c, kvl, g)
        remote(theirs, theirs, osend.at[kvl, g], orecv.at[kvl, g], partner).wait_recv()


def on_device(tokens, queries, norm_gain, w_key, w_value, block_list):
    heads = KVL * GROUP
    cosine, sine = rotary_tables()
    bf16, f32 = jnp.bfloat16, jnp.float32
    dma = pltpu.SemaphoreType.DMA
    out = pl.pallas_call(
        kernel,
        name="layer",
        out_shape=pltpu.VMEM((ROWS, D), bf16),
        in_specs=[pl.BlockSpec(memory_space=pl.ANY)] * 8,
        out_specs=pl.BlockSpec(memory_space=pltpu.VMEM),
        scratch_shapes=[
            pltpu.VMEM((CHUNKS, NX, NY, 2, 128, HD), bf16),
            pltpu.VMEM((PAIR, D), bf16),
            pltpu.VMEM((ROWS, D), bf16),
            pltpu.VMEM((1, D), f32),
            pltpu.VMEM((ROWS, D), bf16),
            pltpu.VMEM((KVL, GROUP, PAIR, HD), bf16),
            pltpu.VMEM((KVL, GROUP, ROWS, HD), bf16),
            pltpu.VMEM((CHUNKS, NZ, PAIR, HD), bf16),
            pltpu.VMEM((2, PAIR, HD), f32),
            pltpu.VMEM((2, PAIR, HD), f32),
            pltpu.VMEM((heads, PLACES, NQB), jnp.int32),
            pltpu.VMEM((heads, PAIR, HD), bf16),
            pltpu.VMEM((NZ, PAIR, HD), bf16),
            pltpu.VMEM((PAIR, PAIR), f32),
            pltpu.VMEM((2, PAIR, LENGTH), f32),
            pltpu.VMEM((2, PAIR, HD), f32),
            pltpu.VMEM((2 * GROUP, PAIR, LENGTH), bf16),
            pltpu.VMEM((2 * GROUP, PAIR, HD), f32),
            pltpu.VMEM((GROUP, PAIR, HD), f32),
            pltpu.VMEM((KVL, GROUP, ROWS, HD), bf16),
            dma((6,)),
            dma((CHUNKS,)),
            dma((CHUNKS,)),
            dma((CHUNKS, 5, 2, 2)),
            dma((CHUNKS,)),
            dma((CHUNKS, 4, 2)),
            dma((2,)),
            dma((2,)),
            dma((KVL, GROUP)),
            dma((KVL, GROUP)),
        ],
        compiler_params=pltpu.CompilerParams(
            collective_id=0, has_side_effects=True, vmem_limit_bytes=56 * 2**20
        ),
        cost_estimate=pl.CostEstimate(
            flops=6_400_000_000, bytes_accessed=6_000_000, transcendentals=8_400_000
        ),
    )(
        tokens[0],
        queries[0],
        norm_gain[None],
        w_key.reshape(2, 128, w_key.shape[1]),
        w_value.reshape(2, 128, w_value.shape[1]),
        block_list[0].transpose(0, 2, 1),
        jnp.asarray(cosine),
        jnp.asarray(sine),
    )
    return out[None]


def solution(mesh):
    in_specs = (
        P("fsdp", "seq", None),
        P("fsdp", "seq", None),
        P(),
        P("fsdp", None),
        P("fsdp", None),
        P("fsdp", None, None, None),
    )
    return jax.shard_map(
        on_device, mesh=mesh, in_specs=in_specs, out_specs=P("fsdp", "seq", None), check_vma=False
    )
```

```python
import functools
import math

import jax
import jax.numpy as jnp
import numpy as np
from jax import lax
from jax.experimental import pallas as pl
from jax.experimental.pallas import tpu as pltpu
from jax.sharding import PartitionSpec as P

MESH = pl.DeviceIdType.MESH
EPS = 1e-05
ROPE_BASE = 500000.0
D = 4096
HD = 128
LENGTH = 2048
NX, NY, NZ = 4, 4, 8
KVL = 4
GROUP = 4
CHUNKS = 2 * KVL
ROWS = 128
PAIR = 2 * ROWS
BLOCK = 64
QB = PAIR // BLOCK
PLACES = 16
NQB = LENGTH // BLOCK
HIDDEN = -1e30
SCALE = math.log2(math.e) / math.sqrt(HD)


def rotary_tables():
    freqs = np.float32(ROPE_BASE) ** (
        -np.arange(HD // 2, dtype=np.float32) * np.float32(2.0 / HD)
    )
    angles = np.arange(LENGTH, dtype=np.float32)[:, None] * freqs.astype(np.float32)[None, :]
    cosine = np.cos(angles.astype(np.float64)).astype(np.float32)
    sine = np.sin(angles.astype(np.float64)).astype(np.float32)
    return np.concatenate([cosine, cosine], 1), np.concatenate([-sine, sine], 1)


def kernel(
    tokens, queries, gain, wk, wv, lists, cos_hbm, sin_hbm, out,
    wbuf, nrm, tok, gn, qin, qrot, qsend, kv, cs, sn, lst, qmask, spread, tri, sbuf, mbuf, pbuf, tbuf, abuf, obuf,
    in_sem, own_sem, wsend, wrecv, zsend, zrecv, core_send, core_recv, osend, orecv,
):
    s = lax.axis_index("seq")
    f = lax.axis_index("fsdp")
    c = lax.rem(s, 2)
    z = lax.div(s, 2)
    x = lax.div(f, NY)
    y = lax.rem(f, NY)
    xn, xp = lax.rem(x + NX - 1, NX), lax.rem(x + 1, NX)
    yn, yp = lax.rem(y + NY - 1, NY), lax.rem(y + 1, NY)
    x2, y2 = lax.rem(x + 2, NX), lax.rem(y + 2, NY)
    x_dev = ((s, xp * NY + y), (s, xn * NY + y))
    y_dev = ((s, x * NY + yp), (s, x * NY + yn))
    z_dev = ((lax.rem(s + 2, 2 * NZ), f), (lax.rem(s + 2 * NZ - 2, 2 * NZ), f))
    partner = (s + 1 - 2 * c, f)
    row0 = pl.multiple_of(c * ROWS, ROWS)
    row1 = pl.multiple_of((1 - c) * ROWS, ROWS)

    def own_copy(t):
        kvl = lax.div(t, 2)
        cols = pl.ds(pl.multiple_of((KVL * c + kvl) * HD, HD), HD)
        return [
            pltpu.make_async_copy(w.at[:, :, cols], wbuf.at[t, x, y], own_sem.at[t])
            for w in (wk, wv)
        ]

    def start_own(t):
        key_copy, value_copy = own_copy(t)

        @pl.when(lax.rem(t, 2) == 0)
        def _():
            key_copy.start()

        @pl.when(lax.rem(t, 2) == 1)
        def _():
            value_copy.start()

    pos = pl.ds(pl.multiple_of(z * PAIR, PAIR), PAIR)
    tok_copy = pltpu.make_async_copy(tokens, tok, in_sem.at[0])
    gain_copy = pltpu.make_async_copy(gain, gn, in_sem.at[1])
    q_copy = pltpu.make_async_copy(queries, qin, in_sem.at[2])
    cos_copy = pltpu.make_async_copy(cos_hbm.at[pos, :], cs.at[0], in_sem.at[3])
    sin_copy = pltpu.make_async_copy(sin_hbm.at[pos, :], sn.at[0], in_sem.at[4])
    list_copy = pltpu.make_async_copy(
        lists.at[pl.ds(c * KVL * GROUP, KVL * GROUP)], lst, in_sem.at[5]
    )

    start_own(0)
    start_own(1)
    tok_copy.start()
    gain_copy.start()
    cos_copy.start()
    sin_copy.start()
    q_copy.start()
    list_copy.start()
    for t in range(2, CHUNKS):
        start_own(t)

    barrier = pltpu.get_barrier_semaphore()
    for device in (*x_dev, *y_dev, *z_dev, partner):
        pl.semaphore_signal(barrier, inc=1, device_id=device, device_id_type=MESH)
    pl.semaphore_wait(barrier, 7)

    def remote(src, dst, send, recv, device):
        return pltpu.make_async_remote_copy(
            src_ref=src, dst_ref=dst, send_sem=send, recv_sem=recv, device_id=device, device_id_type=MESH
        )

    first_dev = (x_dev, y_dev)
    second_dev = (y_dev, x_dev)

    def piece(t, half, step):
        if half == 0:
            return wbuf.at[t, (x, xn, x2, xp)[step], y, 0]
        return wbuf.at[t, x, (y, yn, y2, yp)[step], 1]

    def line(t, half, step, part):
        some = pl.ds(2 * part, 2)
        if half == 0:
            return wbuf.at[t, some, (y, yn, y2, yp)[step], 0]
        return wbuf.at[t, (x, xn, x2, xp)[step], some, 1]

    def rows_of(ref, part):
        return ref.at[pl.ds(64 * part, 64), :]

    def w_send(t, stage, half, d, ref, device):
        remote(ref, ref, wsend.at[t], wrecv.at[t, stage, half, d], device).start()

    def w_wait(t, stage, half, d, ref):
        remote(ref, ref, wsend.at[t], wrecv.at[t, stage, half, d], partner).wait_recv()

    def stage0(t):
        own_copy(t)[0].wait()
        for half in range(2):
            for d in range(2):
                w_send(t, 0, half, d, piece(t, half, 0), first_dev[half][d])

    def stage1(t):
        for half in range(2):
            for d, step in ((0, 1), (1, 3)):
                w_wait(t, 0, half, d, piece(t, half, step))
                w_send(t, 1, half, d, rows_of(piece(t, half, step), d), first_dev[half][d])

    def stage2(t):
        for half in range(2):
            for d in range(2):
                w_wait(t, 1, half, d, rows_of(piece(t, half, 2), d))
            for d in range(2):
                w_send(t, 2, half, d, line(t, half, 0, d), second_dev[half][d])
        for half in range(2):
            for d in range(2):
                w_send(t, 3, half, d, line(t, half, 0, 1 - d), second_dev[half][d])

    def stage3(t):
        for half in range(2):
            for d, step in ((0, 1), (1, 3)):
                w_wait(t, 2, half, d, line(t, half, step, d))
                w_send(t, 4, half, d, line(t, half, step, d), second_dev[half][d])

    def stage4(t):
        for half in range(2):
            for d, step in ((0, 1), (1, 3)):
                w_wait(t, 3, half, d, line(t, half, step, 1 - d))
                w_wait(t, 4, half, d, line(t, half, 2, d))

    def z_slot(t, stage, d):
        if stage == 3:
            return kv.at[t, 4, pl.ds(128 * d, 128), :]
        return kv.at[t, stage + 1 if d == 0 else 7 - stage]

    def z_source(t, stage, d):
        if stage == 3:
            return kv.at[t, 3 if d == 0 else 5, pl.ds(128 * d, 128), :]
        return kv.at[t, stage if d == 0 else (8 - stage) % 8]

    def arrives(stage, d, chip):
        if d == 0:
            return chip >= stage + 1
        return (chip + stage + 1 < NZ // 2) | (chip + stage + 1 >= NZ)

    def leaves(stage, d):
        if d == 0:
            return (z < NZ - 1) & (z >= stage)
        return arrives(stage, d, lax.rem(z + NZ - 1, NZ))

    def z_send(t, stage):
        for d in range(2):

            @pl.when(leaves(stage, d))
            def _():
                remote(
                    z_source(t, stage, d), z_slot(t, stage, d), zsend.at[t], zrecv.at[t, stage, d], z_dev[d]
                ).start()

    def z_wait(t, stage):
        for d in range(2):

            @pl.when(arrives(stage, d, z))
            def _():
                ref = z_slot(t, stage, d)
                remote(ref, ref, zsend.at[t], zrecv.at[t, stage, d], partner).wait_recv()

    def z_sent(t):
        refs = {
            5: wbuf.at[pl.ds(0, 5), 0, 0, 0],
            7: wbuf.at[pl.ds(0, 7), 0, 0, 0],
            8: wbuf.at[pl.ds(0, 8), 0, 0, 0],
            9: qsend.at[pl.ds(0, 3), pl.ds(0, 3)],
            10: spread.at[pl.ds(0, 5)],
        }
        for units, chips in ((5, (7,)), (7, (4,)), (8, (5,)), (9, (0, 3)), (10, (1, 2, 6))):
            here = functools.reduce(jnp.logical_or, [z == chip for chip in chips])

            @pl.when(here)
            def _():
                pltpu.make_async_copy(refs[units], refs[units], zsend.at[t]).wait()

    def clear_rest():
        for r in range(1, NZ):
            used = arrives(r - 1, 0, z) if r <= NZ // 2 else arrives(NZ - 1 - r, 1, z)

            @pl.when(jnp.logical_not(used))
            def _():
                @pl.loop(0, CHUNKS)
                def _(t):
                    kv[t, r] = jnp.zeros((PAIR, HD), jnp.bfloat16)

    nrm_copy = remote(
        nrm.at[pl.ds(row0, ROWS), :], nrm.at[pl.ds(row0, ROWS), :], core_send.at[0], core_recv.at[0], partner
    )
    q_rot_copy = remote(
        qsend, qrot.at[:, :, pl.ds(row0, ROWS), :], core_send.at[1], core_recv.at[1], partner
    )
    nrm_landing = nrm.at[pl.ds(row1, ROWS), :]
    q_landing = qrot.at[:, :, pl.ds(row1, ROWS), :]

    def normalise():
        tok_copy.wait()
        gain_copy.wait()

        @pl.loop(0, ROWS // 16)
        def _(i):
            rows = pl.ds(pl.multiple_of(i * 16, 16), 16)
            wide = tok[rows, :].astype(jnp.float32)
            mean = jnp.sum(wide * wide, axis=-1, keepdims=True) * (1.0 / D)
            normed = wide * lax.rsqrt(mean + EPS) * gn[...]
            nrm[pl.ds(pl.multiple_of(row0 + i * 16, 16), 16), :] = normed.astype(jnp.bfloat16)

        nrm_copy.start()

    def rotate_queries():
        q_copy.wait()
        cos_copy.wait()
        sin_copy.wait()
        cs[1] = jnp.ones((PAIR, HD), jnp.float32)
        sn[1] = jnp.zeros((PAIR, HD), jnp.float32)

        def rotated(head):
            cols = pl.ds(pl.multiple_of(head * HD, HD), HD)
            v = qin[:, cols].astype(jnp.float32)
            turned = v * cs[0, pl.ds(row0, ROWS), :] + pltpu.roll(v, HD // 2, 1) * sn[0, pl.ds(row0, ROWS), :]
            return turned.astype(jnp.bfloat16)

        @pl.loop(0, KVL * GROUP)
        def _(h):
            kvl, g = lax.div(h, GROUP), lax.rem(h, GROUP)
            qsend[kvl, g] = rotated((1 - c) * KVL * GROUP + h)
            qrot[kvl, g, pl.ds(row0, ROWS), :] = rotated(c * KVL * GROUP + h)

        q_rot_copy.start()

    def make_masks():
        list_copy.wait()
        shape = (8, NQB)
        row, lane = (lax.broadcasted_iota(jnp.int32, shape, d) for d in (0, 1))
        mine = (lane == z * QB + row).astype(jnp.bfloat16)
        ids = lst[...].reshape(KVL * GROUP * PLACES, NQB).astype(jnp.float32).astype(jnp.bfloat16)
        picked = lax.dot_general(mine, ids, (((1,), (1,)), ((), ())), preferred_element_type=jnp.float32)
        number = lax.broadcasted_iota(jnp.int32, (8, HD), 1).astype(jnp.float32)
        for h in range(KVL * GROUP):
            hit = picked[:, h * PLACES : h * PLACES + 1] == number
            for place in range(1, PLACES):
                at = h * PLACES + place
                hit = hit | (picked[:, at : at + 1] == number)
            hide = jnp.where(hit, 0.0, HIDDEN)
            for b in range(QB):
                qmask[h, b * BLOCK : (b + 1) * BLOCK, :] = jnp.broadcast_to(
                    hide[b : b + 1, :], (BLOCK, HD)
                ).astype(jnp.bfloat16)
        i = lax.broadcasted_iota(jnp.int32, (PAIR, HD), 0)
        j = lax.broadcasted_iota(jnp.int32, (PAIR, HD), 1)
        for r in range(NZ):
            block = lax.rem(z - r + NZ, NZ) * QB + lax.div(i, BLOCK)
            spread[r] = (block == j).astype(jnp.float32).astype(jnp.bfloat16)
        i = lax.broadcasted_iota(jnp.int32, (PAIR, PAIR), 0)
        j = lax.broadcasted_iota(jnp.int32, (PAIR, PAIR), 1)
        tri[...] = jnp.where(j <= i, 0.0, HIDDEN)

    def project(t):
        acc = jnp.dot(nrm[...], wbuf[t].reshape(D, HD), preferred_element_type=jnp.float32)
        kind = lax.rem(t, 2)
        kv[t, 0] = (acc * cs[kind] + pltpu.roll(acc, HD // 2, 1) * sn[kind]).astype(jnp.bfloat16)

    def score(u, at):
        kvl, g = lax.div(u, GROUP), lax.rem(u, GROUP)
        q = jnp.concatenate([qrot[kvl, g], qmask[u]], 1)
        top = None
        for r in range(NZ):
            keys = jnp.concatenate([kv[2 * kvl, r], spread[r]], 1)
            scores = lax.dot_general(q, keys, (((1,), (1,)), ((), ())), preferred_element_type=jnp.float32)
            if r == 0:
                scores = scores + tri[...]
            sbuf[at, :, r * PAIR : (r + 1) * PAIR] = scores
            here = jnp.maximum(scores[:, :HD], scores[:, HD:])
            top = here if top is None else jnp.maximum(top, here)
        mbuf[at] = jnp.broadcast_to(jnp.max(top, axis=-1, keepdims=True), (PAIR, HD))

    def soften(u, at):
        place = lax.rem(u, 2 * GROUP)
        top, total = mbuf[at], None
        for r in range(LENGTH // HD):
            cols = slice(r * HD, (r + 1) * HD)
            p = jnp.exp2((sbuf[at, :, cols] - top) * SCALE)
            total = p if total is None else total + p
            pbuf[place, :, cols] = p.astype(jnp.bfloat16)
        tbuf[place] = jnp.broadcast_to(jnp.sum(total, axis=-1, keepdims=True), (PAIR, HD))

    def weigh(u):
        kvl, g = lax.div(u, GROUP), lax.rem(u, GROUP)
        values = kv[2 * kvl + 1].reshape(LENGTH, HD)
        place = lax.rem(u, 2 * GROUP)
        acc = jnp.dot(pbuf[place], values, preferred_element_type=jnp.float32)
        put(u, acc)

    def put(u, acc):
        kvl, g = lax.div(u, GROUP), lax.rem(u, GROUP)
        abuf[g] = acc / tbuf[lax.rem(u, 2 * GROUP)]
        obuf[kvl, g] = abuf[g, pl.ds(row1, ROWS), :].astype(jnp.bfloat16)
        cols = pl.ds(pl.multiple_of((c * KVL * GROUP + u) * HD, HD), HD)
        out[:, cols] = abuf[g, pl.ds(row0, ROWS), :].astype(jnp.bfloat16)

    def out_cols(core, kvl, g):
        return out.at[:, pl.ds(pl.multiple_of(((core * KVL + kvl) * GROUP + g) * HD, HD), HD)]

    def out_remote(kvl, g):
        return remote(
            obuf.at[kvl, g], out_cols(c, kvl, g), osend.at[kvl, g], orecv.at[kvl, g], partner
        )

    def pair_scores(m):
        for i in range(2):
            score(2 * m + i, i)
        for i in range(2):
            soften(2 * m + i, i)

    def pair_values_first(m):
        for i in range(2):
            u = 2 * m + i
            kvl, g, place = u // GROUP, u % GROUP, u % (2 * GROUP)
            acc = None
            for low, high in ((0, NZ // 2), (NZ // 2 + 1, NZ)):
                values = kv[2 * kvl + 1, low:high].reshape((high - low) * PAIR, HD)
                weights = pbuf[place, :, low * PAIR : high * PAIR]
                part = jnp.dot(weights, values, preferred_element_type=jnp.float32)
                acc = part if acc is None else acc + part
            abuf[g] = acc

    def pair_values_last(m):
        for i in range(2):
            u = 2 * m + i
            kvl, g, place = u // GROUP, u % GROUP, u % (2 * GROUP)
            half = NZ // 2
            weights = pbuf[place, :, half * PAIR : (half + 1) * PAIR]
            part = jnp.dot(weights, kv[2 * kvl + 1, half], preferred_element_type=jnp.float32)
            put(u, abuf[g] + part)
            out_remote(kvl, g).start()

    def pair_values(m):
        for i in range(2):
            weigh(2 * m + i)
        for i in range(2):
            u = 2 * m + i
            out_remote(lax.div(u, GROUP), lax.rem(u, GROUP)).start()

    def around(stage):
        def step(t):
            z_wait(t, stage - 1)
            if stage < 4:
                z_send(t, stage)

        return step

    def compute(t):
        stage4(t)

        @pl.when(t == 0)
        def _():
            remote(nrm_landing, nrm_landing, core_send.at[0], core_recv.at[0], partner).wait_recv()

        project(t)
        z_send(t, 0)

    stage0(0)
    stage0(1)
    stage0(2)
    stage0(3)
    stage0(4)
    normalise()
    stage1(0)
    stage0(5)
    stage0(6)
    stage1(1)
    stage1(2)
    stage1(3)
    stage2(0)

    def slot(n, carry):
        def when(t, what, low=0, high=CHUNKS):
            @pl.when((t >= low) & (t < high))
            def _():
                what(t)

        when(n + 1, stage2)
        when(n - 3, around(1))

        @pl.when(n == 0)
        def _():
            rotate_queries()

        @pl.when(n == 3)
        def _():
            make_masks()
            clear_rest()

        @pl.when(n == 7)
        def _():
            remote(q_landing, q_landing, core_send.at[1], core_recv.at[1], partner).wait_recv()

        when(n - 7, pair_scores)
        when(n - 4, around(2))
        when(n - 5, around(3))
        when(n + 7, stage0)
        when(n, stage3)
        when(n + 4, stage1)
        when(n - 1, compute)
        when(n - 6, around(4))
        return carry

    lax.fori_loop(0, 9, slot, 0)

    pair_scores(2)
    around(1)(6)
    pair_values(0)
    around(2)(5)
    pair_scores(3)
    around(4)(3)
    pair_values(1)
    around(3)(4)
    around(1)(7)
    pair_values(2)
    pair_values(3)
    around(2)(6)
    around(3)(5)
    around(4)(4)
    pair_scores(4)
    around(2)(7)
    pair_scores(5)
    around(3)(6)
    around(4)(5)
    pair_values(4)
    pair_values(5)
    around(3)(7)
    around(4)(6)
    pair_scores(6)
    pair_scores(7)
    around(4)(7)
    pair_values_first(6)
    pair_values_last(6)
    pair_values_first(7)
    pair_values_last(7)

    nrm_copy.wait_send()
    q_rot_copy.wait_send()

    @pl.loop(0, CHUNKS)
    def _(t):
        sent = nrm.at[:, pl.ds(0, 15 * HD)]
        pltpu.make_async_copy(sent, sent, wsend.at[t]).wait()
        z_sent(t)

    @pl.loop(0, KVL * GROUP)
    def _(u):
        kvl, g = lax.div(u, GROUP), lax.rem(u, GROUP)
        out_remote(kvl, g).wait_send()
        theirs = out_cols(1 - c, kvl, g)
        remote(theirs, theirs, osend.at[kvl, g], orecv.at[kvl, g], partner).wait_recv()


def on_device(tokens, queries, norm_gain, w_key, w_value, block_list):
    heads = KVL * GROUP
    cosine, sine = rotary_tables()
    bf16, f32 = jnp.bfloat16, jnp.float32
    dma = pltpu.SemaphoreType.DMA
    out = pl.pallas_call(
        kernel,
        name="layer",
        out_shape=pltpu.VMEM((ROWS, D), bf16),
        in_specs=[pl.BlockSpec(memory_space=pl.ANY)] * 8,
        out_specs=pl.BlockSpec(memory_space=pltpu.VMEM),
        scratch_shapes=[
            pltpu.VMEM((CHUNKS, NX, NY, 2, 128, HD), bf16),
            pltpu.VMEM((PAIR, D), bf16),
            pltpu.VMEM((ROWS, D), bf16),
            pltpu.VMEM((1, D), f32),
            pltpu.VMEM((ROWS, D), bf16),
            pltpu.VMEM((KVL, GROUP, PAIR, HD), bf16),
            pltpu.VMEM((KVL, GROUP, ROWS, HD), bf16),
            pltpu.VMEM((CHUNKS, NZ, PAIR, HD), bf16),
            pltpu.VMEM((2, PAIR, HD), f32),
            pltpu.VMEM((2, PAIR, HD), f32),
            pltpu.VMEM((heads, PLACES, NQB), jnp.int32),
            pltpu.VMEM((heads, PAIR, HD), bf16),
            pltpu.VMEM((NZ, PAIR, HD), bf16),
            pltpu.VMEM((PAIR, PAIR), f32),
            pltpu.VMEM((2, PAIR, LENGTH), f32),
            pltpu.VMEM((2, PAIR, HD), f32),
            pltpu.VMEM((2 * GROUP, PAIR, LENGTH), bf16),
            pltpu.VMEM((2 * GROUP, PAIR, HD), f32),
            pltpu.VMEM((GROUP, PAIR, HD), f32),
            pltpu.VMEM((KVL, GROUP, ROWS, HD), bf16),
            dma((6,)),
            dma((CHUNKS,)),
            dma((CHUNKS,)),
            dma((CHUNKS, 5, 2, 2)),
            dma((CHUNKS,)),
            dma((CHUNKS, 4, 2)),
            dma((2,)),
            dma((2,)),
            dma((KVL, GROUP)),
            dma((KVL, GROUP)),
        ],
        compiler_params=pltpu.CompilerParams(
            collective_id=0, has_side_effects=True, vmem_limit_bytes=56 * 2**20
        ),
        cost_estimate=pl.CostEstimate(
            flops=6_400_000_000, bytes_accessed=6_000_000, transcendentals=8_400_000
        ),
    )(
        tokens[0],
        queries[0],
        norm_gain[None],
        w_key.reshape(2, 128, w_key.shape[1]),
        w_value.reshape(2, 128, w_value.shape[1]),
        block_list[0].transpose(0, 2, 1),
        jnp.asarray(cosine),
        jnp.asarray(sine),
    )
    return out[None]


def solution(mesh):
    in_specs = (
        P("fsdp", "seq", None),
        P("fsdp", "seq", None),
        P(),
        P("fsdp", None),
        P("fsdp", None),
        P("fsdp", None, None, None),
    )
    return jax.shard_map(
        on_device, mesh=mesh, in_specs=in_specs, out_specs=P("fsdp", "seq", None), check_vma=False
    )
```

```python
import functools
import math

import jax
import jax.numpy as jnp
import numpy as np
from jax import lax
from jax.experimental import pallas as pl
from jax.experimental.pallas import tpu as pltpu
from jax.sharding import PartitionSpec as P

MESH = pl.DeviceIdType.MESH
EPS = 1e-05
ROPE_BASE = 500000.0
D = 4096
HD = 128
LENGTH = 2048
NX, NY, NZ = 4, 4, 8
KVL = 4
GROUP = 4
CHUNKS = 2 * KVL
ROWS = 128
PAIR = 2 * ROWS
BLOCK = 64
QB = PAIR // BLOCK
PLACES = 16
NQB = LENGTH // BLOCK
HIDDEN = -1e30
SCALE = math.log2(math.e) / math.sqrt(HD)


def rotary_tables():
    freqs = np.float32(ROPE_BASE) ** (
        -np.arange(HD // 2, dtype=np.float32) * np.float32(2.0 / HD)
    )
    angles = np.arange(LENGTH, dtype=np.float32)[:, None] * freqs.astype(np.float32)[None, :]
    cosine = np.cos(angles.astype(np.float64)).astype(np.float32)
    sine = np.sin(angles.astype(np.float64)).astype(np.float32)
    return np.concatenate([cosine, cosine], 1), np.concatenate([-sine, sine], 1)


def kernel(
    tokens, queries, gain, wk, wv, lists, cos_hbm, sin_hbm, out,
    wbuf, nrm, tok, gn, qin, qrot, qsend, kv, cs, sn, lst, qmask, spread, tri, sbuf, mbuf, pbuf, tbuf, abuf, obuf,
    in_sem, own_sem, wsend, wrecv, zsend, zrecv, core_send, core_recv, osend, orecv,
):
    s = lax.axis_index("seq")
    f = lax.axis_index("fsdp")
    c = lax.rem(s, 2)
    z = lax.div(s, 2)
    x = lax.div(f, NY)
    y = lax.rem(f, NY)
    xn, xp = lax.rem(x + NX - 1, NX), lax.rem(x + 1, NX)
    yn, yp = lax.rem(y + NY - 1, NY), lax.rem(y + 1, NY)
    x2, y2 = lax.rem(x + 2, NX), lax.rem(y + 2, NY)
    x_dev = ((s, xp * NY + y), (s, xn * NY + y))
    y_dev = ((s, x * NY + yp), (s, x * NY + yn))
    z_dev = ((lax.rem(s + 2, 2 * NZ), f), (lax.rem(s + 2 * NZ - 2, 2 * NZ), f))
    partner = (s + 1 - 2 * c, f)
    row0 = pl.multiple_of(c * ROWS, ROWS)
    row1 = pl.multiple_of((1 - c) * ROWS, ROWS)

    def own_copy(t):
        kvl = lax.div(t, 2)
        cols = pl.ds(pl.multiple_of((KVL * c + kvl) * HD, HD), HD)
        return [
            pltpu.make_async_copy(w.at[:, :, cols], wbuf.at[t, x, y], own_sem.at[t])
            for w in (wk, wv)
        ]

    def start_own(t):
        key_copy, value_copy = own_copy(t)

        @pl.when(lax.rem(t, 2) == 0)
        def _():
            key_copy.start()

        @pl.when(lax.rem(t, 2) == 1)
        def _():
            value_copy.start()

    pos = pl.ds(pl.multiple_of(z * PAIR, PAIR), PAIR)
    tok_copy = pltpu.make_async_copy(tokens, tok, in_sem.at[0])
    gain_copy = pltpu.make_async_copy(gain, gn, in_sem.at[1])
    q_copy = pltpu.make_async_copy(queries, qin, in_sem.at[2])
    cos_copy = pltpu.make_async_copy(cos_hbm.at[pos, :], cs.at[0], in_sem.at[3])
    sin_copy = pltpu.make_async_copy(sin_hbm.at[pos, :], sn.at[0], in_sem.at[4])
    list_copy = pltpu.make_async_copy(
        lists.at[pl.ds(c * KVL * GROUP, KVL * GROUP)], lst, in_sem.at[5]
    )

    start_own(0)
    start_own(1)
    tok_copy.start()
    gain_copy.start()
    cos_copy.start()
    sin_copy.start()
    q_copy.start()
    list_copy.start()
    for t in range(2, CHUNKS):
        start_own(t)

    barrier = pltpu.get_barrier_semaphore()
    for device in (*x_dev, *y_dev, *z_dev, partner):
        pl.semaphore_signal(barrier, inc=1, device_id=device, device_id_type=MESH)
    pl.semaphore_wait(barrier, 7)

    def remote(src, dst, send, recv, device):
        return pltpu.make_async_remote_copy(
            src_ref=src, dst_ref=dst, send_sem=send, recv_sem=recv, device_id=device, device_id_type=MESH
        )

    first_dev = (x_dev, y_dev)
    second_dev = (y_dev, x_dev)

    def piece(t, half, step):
        if half == 0:
            return wbuf.at[t, (x, xn, x2, xp)[step], y, 0]
        return wbuf.at[t, x, (y, yn, y2, yp)[step], 1]

    def line(t, half, step, part):
        some = pl.ds(2 * part, 2)
        if half == 0:
            return wbuf.at[t, some, (y, yn, y2, yp)[step], 0]
        return wbuf.at[t, (x, xn, x2, xp)[step], some, 1]

    def rows_of(ref, part):
        return ref.at[pl.ds(64 * part, 64), :]

    def w_send(t, stage, half, d, ref, device):
        remote(ref, ref, wsend.at[t], wrecv.at[t, stage, half, d], device).start()

    def w_wait(t, stage, half, d, ref):
        remote(ref, ref, wsend.at[t], wrecv.at[t, stage, half, d], partner).wait_recv()

    def stage0(t):
        own_copy(t)[0].wait()
        for half in range(2):
            for d in range(2):
                w_send(t, 0, half, d, piece(t, half, 0), first_dev[half][d])

    def stage1(t):
        for half in range(2):
            for d, step in ((0, 1), (1, 3)):
                w_wait(t, 0, half, d, piece(t, half, step))
                w_send(t, 1, half, d, rows_of(piece(t, half, step), d), first_dev[half][d])

    def stage2(t):
        for half in range(2):
            for d in range(2):
                w_wait(t, 1, half, d, rows_of(piece(t, half, 2), d))
            for d in range(2):
                w_send(t, 2, half, d, line(t, half, 0, d), second_dev[half][d])
        for half in range(2):
            for d in range(2):
                w_send(t, 3, half, d, line(t, half, 0, 1 - d), second_dev[half][d])

    def stage3(t):
        for half in range(2):
            for d, step in ((0, 1), (1, 3)):
                w_wait(t, 2, half, d, line(t, half, step, d))
                w_send(t, 4, half, d, line(t, half, step, d), second_dev[half][d])

    def stage4(t):
        for half in range(2):
            for d, step in ((0, 1), (1, 3)):
                w_wait(t, 3, half, d, line(t, half, step, 1 - d))
                w_wait(t, 4, half, d, line(t, half, 2, d))

    def z_slot(t, stage, d):
        if stage == 3:
            return kv.at[t, 4, pl.ds(128 * d, 128), :]
        return kv.at[t, stage + 1 if d == 0 else 7 - stage]

    def z_source(t, stage, d):
        if stage == 3:
            return kv.at[t, 3 if d == 0 else 5, pl.ds(128 * d, 128), :]
        return kv.at[t, stage if d == 0 else (8 - stage) % 8]

    def arrives(stage, d, chip):
        if d == 0:
            return chip >= stage + 1
        return (chip + stage + 1 < NZ // 2) | (chip + stage + 1 >= NZ)

    def leaves(stage, d):
        if d == 0:
            return (z < NZ - 1) & (z >= stage)
        return arrives(stage, d, lax.rem(z + NZ - 1, NZ))

    def z_send(t, stage):
        for d in range(2):

            @pl.when(leaves(stage, d))
            def _():
                remote(
                    z_source(t, stage, d), z_slot(t, stage, d), zsend.at[t], zrecv.at[t, stage, d], z_dev[d]
                ).start()

    def z_wait(t, stage):
        for d in range(2):

            @pl.when(arrives(stage, d, z))
            def _():
                ref = z_slot(t, stage, d)
                remote(ref, ref, zsend.at[t], zrecv.at[t, stage, d], partner).wait_recv()

    def z_sent(t):
        refs = {
            5: wbuf.at[pl.ds(0, 5), 0, 0, 0],
            7: wbuf.at[pl.ds(0, 7), 0, 0, 0],
            8: wbuf.at[pl.ds(0, 8), 0, 0, 0],
            9: qsend.at[pl.ds(0, 3), pl.ds(0, 3)],
            10: spread.at[pl.ds(0, 5)],
        }
        for units, chips in ((5, (7,)), (7, (4,)), (8, (5,)), (9, (0, 3)), (10, (1, 2, 6))):
            here = functools.reduce(jnp.logical_or, [z == chip for chip in chips])

            @pl.when(here)
            def _():
                pltpu.make_async_copy(refs[units], refs[units], zsend.at[t]).wait()

    def clear_rest():
        for r in range(1, NZ):
            used = arrives(r - 1, 0, z) if r <= NZ // 2 else arrives(NZ - 1 - r, 1, z)

            @pl.when(jnp.logical_not(used))
            def _():
                @pl.loop(0, CHUNKS)
                def _(t):
                    kv[t, r] = jnp.zeros((PAIR, HD), jnp.bfloat16)

    nrm_copy = remote(
        nrm.at[pl.ds(row0, ROWS), :], nrm.at[pl.ds(row0, ROWS), :], core_send.at[0], core_recv.at[0], partner
    )
    q_rot_copy = remote(
        qsend, qrot.at[:, :, pl.ds(row0, ROWS), :], core_send.at[1], core_recv.at[1], partner
    )
    nrm_landing = nrm.at[pl.ds(row1, ROWS), :]
    q_landing = qrot.at[:, :, pl.ds(row1, ROWS), :]

    def normalise():
        tok_copy.wait()
        gain_copy.wait()

        @pl.loop(0, ROWS // 16)
        def _(i):
            rows = pl.ds(pl.multiple_of(i * 16, 16), 16)
            wide = tok[rows, :].astype(jnp.float32)
            mean = jnp.sum(wide * wide, axis=-1, keepdims=True) * (1.0 / D)
            normed = wide * lax.rsqrt(mean + EPS) * gn[...]
            nrm[pl.ds(pl.multiple_of(row0 + i * 16, 16), 16), :] = normed.astype(jnp.bfloat16)

        nrm_copy.start()

    def rotate_queries():
        q_copy.wait()
        cos_copy.wait()
        sin_copy.wait()
        cs[1] = jnp.ones((PAIR, HD), jnp.float32)
        sn[1] = jnp.zeros((PAIR, HD), jnp.float32)

        def rotated(head):
            cols = pl.ds(pl.multiple_of(head * HD, HD), HD)
            v = qin[:, cols].astype(jnp.float32)
            turned = v * cs[0, pl.ds(row0, ROWS), :] + pltpu.roll(v, HD // 2, 1) * sn[0, pl.ds(row0, ROWS), :]
            return turned.astype(jnp.bfloat16)

        @pl.loop(0, KVL * GROUP)
        def _(h):
            kvl, g = lax.div(h, GROUP), lax.rem(h, GROUP)
            qsend[kvl, g] = rotated((1 - c) * KVL * GROUP + h)
            qrot[kvl, g, pl.ds(row0, ROWS), :] = rotated(c * KVL * GROUP + h)

        q_rot_copy.start()

    def make_masks():
        list_copy.wait()
        shape = (8, NQB)
        row, lane = (lax.broadcasted_iota(jnp.int32, shape, d) for d in (0, 1))
        mine = (lane == z * QB + row).astype(jnp.bfloat16)
        ids = lst[...].reshape(KVL * GROUP * PLACES, NQB).astype(jnp.float32).astype(jnp.bfloat16)
        picked = lax.dot_general(mine, ids, (((1,), (1,)), ((), ())), preferred_element_type=jnp.float32)
        number = lax.broadcasted_iota(jnp.int32, (8, HD), 1).astype(jnp.float32)
        for h in range(KVL * GROUP):
            hit = picked[:, h * PLACES : h * PLACES + 1] == number
            for place in range(1, PLACES):
                at = h * PLACES + place
                hit = hit | (picked[:, at : at + 1] == number)
            hide = jnp.where(hit, 0.0, HIDDEN)
            for b in range(QB):
                qmask[h, b * BLOCK : (b + 1) * BLOCK, :] = jnp.broadcast_to(
                    hide[b : b + 1, :], (BLOCK, HD)
                ).astype(jnp.bfloat16)
        i = lax.broadcasted_iota(jnp.int32, (PAIR, HD), 0)
        j = lax.broadcasted_iota(jnp.int32, (PAIR, HD), 1)
        for r in range(NZ):
            block = lax.rem(z - r + NZ, NZ) * QB + lax.div(i, BLOCK)
            spread[r] = (block == j).astype(jnp.float32).astype(jnp.bfloat16)
        i = lax.broadcasted_iota(jnp.int32, (PAIR, PAIR), 0)
        j = lax.broadcasted_iota(jnp.int32, (PAIR, PAIR), 1)
        tri[...] = jnp.where(j <= i, 0.0, HIDDEN)

    def project(t):
        acc = jnp.dot(nrm[...], wbuf[t].reshape(D, HD), preferred_element_type=jnp.float32)
        kind = lax.rem(t, 2)
        kv[t, 0] = (acc * cs[kind] + pltpu.roll(acc, HD // 2, 1) * sn[kind]).astype(jnp.bfloat16)

    def score(u, at):
        kvl, g = lax.div(u, GROUP), lax.rem(u, GROUP)
        q = jnp.concatenate([qrot[kvl, g], qmask[u]], 1)
        top = None
        for r in range(NZ):
            keys = jnp.concatenate([kv[2 * kvl, r], spread[r]], 1)
            scores = lax.dot_general(q, keys, (((1,), (1,)), ((), ())), preferred_element_type=jnp.float32)
            if r == 0:
                scores = scores + tri[...]
            sbuf[at, :, r * PAIR : (r + 1) * PAIR] = scores
            here = jnp.maximum(scores[:, :HD], scores[:, HD:])
            top = here if top is None else jnp.maximum(top, here)
        mbuf[at] = jnp.broadcast_to(jnp.max(top, axis=-1, keepdims=True), (PAIR, HD))

    def soften(u, at):
        place = lax.rem(u, 2 * GROUP)
        top, total = mbuf[at], None
        for r in range(LENGTH // HD):
            cols = slice(r * HD, (r + 1) * HD)
            p = jnp.exp2((sbuf[at, :, cols] - top) * SCALE)
            total = p if total is None else total + p
            pbuf[place, :, cols] = p.astype(jnp.bfloat16)
        tbuf[place] = jnp.broadcast_to(jnp.sum(total, axis=-1, keepdims=True), (PAIR, HD))

    def weigh(u):
        kvl, g = lax.div(u, GROUP), lax.rem(u, GROUP)
        values = kv[2 * kvl + 1].reshape(LENGTH, HD)
        place = lax.rem(u, 2 * GROUP)
        acc = jnp.dot(pbuf[place], values, preferred_element_type=jnp.float32)
        put(u, acc)

    def put(u, acc):
        kvl, g = lax.div(u, GROUP), lax.rem(u, GROUP)
        abuf[g] = acc / tbuf[lax.rem(u, 2 * GROUP)]
        obuf[kvl, g] = abuf[g, pl.ds(row1, ROWS), :].astype(jnp.bfloat16)
        cols = pl.ds(pl.multiple_of((c * KVL * GROUP + u) * HD, HD), HD)
        out[:, cols] = abuf[g, pl.ds(row0, ROWS), :].astype(jnp.bfloat16)

    def out_cols(core, kvl, g):
        return out.at[:, pl.ds(pl.multiple_of(((core * KVL + kvl) * GROUP + g) * HD, HD), HD)]

    def out_remote(kvl, g):
        return remote(
            obuf.at[kvl, g], out_cols(c, kvl, g), osend.at[kvl, g], orecv.at[kvl, g], partner
        )

    def pair_scores(m):
        for i in range(2):
            score(2 * m + i, i)
        for i in range(2):
            soften(2 * m + i, i)

    def pair_values_first(m):
        for i in range(2):
            u = 2 * m + i
            kvl, g, place = u // GROUP, u % GROUP, u % (2 * GROUP)
            acc = None
            for low, high in ((0, NZ // 2), (NZ // 2 + 1, NZ)):
                values = kv[2 * kvl + 1, low:high].reshape((high - low) * PAIR, HD)
                weights = pbuf[place, :, low * PAIR : high * PAIR]
                part = jnp.dot(weights, values, preferred_element_type=jnp.float32)
                acc = part if acc is None else acc + part
            abuf[g] = acc

    def pair_values_last(m):
        for i in range(2):
            u = 2 * m + i
            kvl, g, place = u // GROUP, u % GROUP, u % (2 * GROUP)
            half = NZ // 2
            weights = pbuf[place, :, half * PAIR : (half + 1) * PAIR]
            part = jnp.dot(weights, kv[2 * kvl + 1, half], preferred_element_type=jnp.float32)
            put(u, abuf[g] + part)
            out_remote(kvl, g).start()

    def pair_values(m):
        for i in range(2):
            weigh(2 * m + i)
        for i in range(2):
            u = 2 * m + i
            out_remote(lax.div(u, GROUP), lax.rem(u, GROUP)).start()

    def around(stage):
        def step(t):
            z_wait(t, stage - 1)
            if stage < 4:
                z_send(t, stage)

        return step

    def compute(t):
        stage4(t)

        @pl.when(t == 0)
        def _():
            remote(nrm_landing, nrm_landing, core_send.at[0], core_recv.at[0], partner).wait_recv()

        project(t)
        z_send(t, 0)

    stage0(0)
    stage0(1)
    stage0(2)
    stage0(3)
    stage0(4)
    normalise()
    stage1(0)
    stage0(5)
    stage0(6)
    stage1(1)
    stage1(2)
    stage1(3)
    stage2(0)

    def slot(n, carry):
        def when(t, what, low=0, high=CHUNKS):
            @pl.when((t >= low) & (t < high))
            def _():
                what(t)

        when(n + 1, stage2)
        when(n - 3, around(1))

        @pl.when(n == 0)
        def _():
            rotate_queries()

        @pl.when(n == 3)
        def _():
            make_masks()
            clear_rest()

        @pl.when(n == 7)
        def _():
            remote(q_landing, q_landing, core_send.at[1], core_recv.at[1], partner).wait_recv()

        when(n - 7, pair_scores)
        when(n - 4, around(2))
        when(n - 5, around(3))
        when(n + 7, stage0)
        when(n, stage3)
        when(n + 4, stage1)
        when(n - 1, compute)
        when(n - 6, around(4))
        return carry

    lax.fori_loop(0, 9, slot, 0)

    pair_scores(2)
    around(1)(6)
    pair_values(0)
    around(2)(5)
    pair_scores(3)
    around(4)(3)
    pair_values(1)
    around(3)(4)
    around(1)(7)
    pair_values(2)
    pair_values(3)
    around(2)(6)
    around(3)(5)
    around(4)(4)
    pair_scores(4)
    around(2)(7)
    pair_scores(5)
    around(3)(6)
    around(4)(5)
    pair_values(4)
    pair_values(5)
    around(3)(7)
    around(4)(6)
    pair_scores(6)
    pair_scores(7)
    pair_values_first(6)
    pair_values_first(7)
    nrm_copy.wait_send()
    q_rot_copy.wait_send()
    around(4)(7)
    pair_values_last(6)
    pair_values_last(7)

    @pl.loop(0, CHUNKS)
    def _(t):
        sent = nrm.at[:, pl.ds(0, 15 * HD)]
        pltpu.make_async_copy(sent, sent, wsend.at[t]).wait()
        z_sent(t)

    @pl.loop(0, KVL * GROUP)
    def _(u):
        kvl, g = lax.div(u, GROUP), lax.rem(u, GROUP)
        out_remote(kvl, g).wait_send()
        theirs = out_cols(1 - c, kvl, g)
        remote(theirs, theirs, osend.at[kvl, g], orecv.at[kvl, g], partner).wait_recv()


def on_device(tokens, queries, norm_gain, w_key, w_value, block_list):
    heads = KVL * GROUP
    cosine, sine = rotary_tables()
    bf16, f32 = jnp.bfloat16, jnp.float32
    dma = pltpu.SemaphoreType.DMA
    out = pl.pallas_call(
        kernel,
        name="layer",
        out_shape=pltpu.VMEM((ROWS, D), bf16),
        in_specs=[pl.BlockSpec(memory_space=pl.ANY)] * 8,
        out_specs=pl.BlockSpec(memory_space=pltpu.VMEM),
        scratch_shapes=[
            pltpu.VMEM((CHUNKS, NX, NY, 2, 128, HD), bf16),
            pltpu.VMEM((PAIR, D), bf16),
            pltpu.VMEM((ROWS, D), bf16),
            pltpu.VMEM((1, D), f32),
            pltpu.VMEM((ROWS, D), bf16),
            pltpu.VMEM((KVL, GROUP, PAIR, HD), bf16),
            pltpu.VMEM((KVL, GROUP, ROWS, HD), bf16),
            pltpu.VMEM((CHUNKS, NZ, PAIR, HD), bf16),
            pltpu.VMEM((2, PAIR, HD), f32),
            pltpu.VMEM((2, PAIR, HD), f32),
            pltpu.VMEM((heads, PLACES, NQB), jnp.int32),
            pltpu.VMEM((heads, PAIR, HD), bf16),
            pltpu.VMEM((NZ, PAIR, HD), bf16),
            pltpu.VMEM((PAIR, PAIR), f32),
            pltpu.VMEM((2, PAIR, LENGTH), f32),
            pltpu.VMEM((2, PAIR, HD), f32),
            pltpu.VMEM((2 * GROUP, PAIR, LENGTH), bf16),
            pltpu.VMEM((2 * GROUP, PAIR, HD), f32),
            pltpu.VMEM((GROUP, PAIR, HD), f32),
            pltpu.VMEM((KVL, GROUP, ROWS, HD), bf16),
            dma((6,)),
            dma((CHUNKS,)),
            dma((CHUNKS,)),
            dma((CHUNKS, 5, 2, 2)),
            dma((CHUNKS,)),
            dma((CHUNKS, 4, 2)),
            dma((2,)),
            dma((2,)),
            dma((KVL, GROUP)),
            dma((KVL, GROUP)),
        ],
        compiler_params=pltpu.CompilerParams(
            collective_id=0, has_side_effects=True, vmem_limit_bytes=56 * 2**20
        ),
        cost_estimate=pl.CostEstimate(
            flops=6_400_000_000, bytes_accessed=6_000_000, transcendentals=8_400_000
        ),
    )(
        tokens[0],
        queries[0],
        norm_gain[None],
        w_key.reshape(2, 128, w_key.shape[1]),
        w_value.reshape(2, 128, w_value.shape[1]),
        block_list[0].transpose(0, 2, 1),
        jnp.asarray(cosine),
        jnp.asarray(sine),
    )
    return out[None]


def solution(mesh):
    in_specs = (
        P("fsdp", "seq", None),
        P("fsdp", "seq", None),
        P(),
        P("fsdp", None),
        P("fsdp", None),
        P("fsdp", None, None, None),
    )
    return jax.shard_map(
        on_device, mesh=mesh, in_specs=in_specs, out_specs=P("fsdp", "seq", None), check_vma=False
    )
```
